512 devices in a mesh: visit: 8 (over x, core), patch: 64 (over y, z).
Axes of the slice: x: 4, y: 8, z: 8, core: 2. Of those that a mesh axis runs over, the one named last changes fastest.
Arguments:
- template: bfloat16 [64, 8, 16, 2304], P('patch', 'visit'), may hold values from -5 to 5
- science: bfloat16 [8, 64, 8, 16, 1024], P('visit', 'patch'), may hold values from -12 to 12
- weight: bfloat16 [8, 64, 8, 16], P('visit', 'patch'), may hold values from 0.5 to 2
- stamp_patch: int32 [64, 8, 16], P('patch', 'visit'), may hold values from 0 to 63, as said below
- basis_across: float32 [43, 17], replicated, may hold values from -0.6 to 0.6
- basis_down: float32 [43, 17], replicated, may hold values from -0.6 to 0.6
Outputs:
- kernel_coef: float32 [8, 64, 43], P('visit', 'patch')
- residual: float32 [8, 64, 8, 16], P(None, 'patch', 'visit')
The draws below stay inside these ranges and needn't reach their ends.
Inputs may be any that keep to these rules, and one draw needn't show every extreme that they name: `stamp_patch`: the stamps of detector d lie in patches d - 1, d, d + 1, d + 2 (modulo 64), patch d always among them; in every draw some detector has stamps in its patch d - 1. Every one of the 64 patches holds at least one stamp.
All inputs are finite; a program needn't handle non-finite values.
Results may differ from the reference program's by a relative error of at most 0.0057.
Values may be sent and summed in bfloat16 or wider, within the bound.
A program may use at most 128 MiB of HBM per device.

```python
import math
import jax
import jax.numpy as jnp
from jax import lax

STAMP = 32
KS = 17
NB = 43
S_LOC = 16
VISITS = 8
DETS = 64
SUBS = 8
PATCHES = 64
STAMPS = 8192
TS = 48
PIX = 1024
TPIX = 2304


def log_uniform(key, shape, lower, upper):
    return jnp.exp(jax.random.uniform(key, shape, jnp.float32, jnp.log(lower), jnp.log(upper)))


def profile(coords, centre, width):
    scaled = (coords - centre[..., None]) / width[..., None]
    return jnp.exp(-0.5 * scaled * scaled)


def stamp_fields(key):
    shape = (DETS, SUBS, S_LOC)
    coords = jnp.arange(TS, dtype=jnp.float32) - 0.5 * (TS - 1)
    base_width = log_uniform(jax.random.fold_in(key, 41), (DETS, 1, 1), 1.3, 2.6)
    bright = log_uniform(jax.random.fold_in(key, 42), shape, 0.5, 4.5)
    sky = jax.random.uniform(jax.random.fold_in(key, 43), shape, jnp.float32, 0.05, 0.5)
    noise = 0.3 * jax.random.normal(jax.random.fold_in(key, 46), shape + (TS, TS), jnp.float32)
    background = sky[..., None, None]
    width = base_width * jax.random.uniform(jax.random.fold_in(key, 47), shape, jnp.float32, 0.85, 1.15)
    centre_x = jax.random.uniform(jax.random.fold_in(key, 48), shape, jnp.float32, -4.0, 4.0)
    centre_y = jax.random.uniform(jax.random.fold_in(key, 49), shape, jnp.float32, -4.0, 4.0)
    other_x = jax.random.uniform(jax.random.fold_in(key, 50), shape, jnp.float32, -18.0, 18.0)
    other_y = jax.random.uniform(jax.random.fold_in(key, 51), shape, jnp.float32, -18.0, 18.0)
    other_bright = log_uniform(jax.random.fold_in(key, 52), shape, 0.1, 1.5)
    star = bright[..., None, None] * profile(coords, centre_y, width)[..., :, None] * profile(coords, centre_x, width)[..., None, :]
    companion = other_bright[..., None, None] * profile(coords, other_y, width)[..., :, None] * profile(coords, other_x, width)[..., None, :]
    fields = background + star + companion + noise
    return jnp.clip(fields, -5.0, 5.0)


def draw_template(key, part):
    return stamp_fields(key).reshape(DETS, SUBS, S_LOC, TS * TS).astype(jnp.bfloat16)


def draw_science(key, part):
    fields = stamp_fields(key)
    margin = (KS - 1) // 2
    centre = fields[:, :, :, margin:margin + STAMP, margin:margin + STAMP]
    place = (jnp.arange(DETS)[:, None] * SUBS + jnp.arange(SUBS)[None, :]).astype(jnp.float32)
    place = place / max(DETS * SUBS - 1, 1)
    slope = jnp.exp(place * jnp.log(3.0))
    visit_gain = jax.random.uniform(jax.random.fold_in(key, 21), (VISITS,), jnp.float32, 0.6, 1.2)
    jitter = jax.random.uniform(jax.random.fold_in(key, 22), (VISITS, DETS, SUBS, S_LOC), jnp.float32, 0.85, 1.15)
    gain = visit_gain[:, None, None, None] * slope[None, :, :, None] * jitter
    noise_shape = (VISITS, DETS, SUBS, S_LOC, STAMP, STAMP)
    noise = 0.5 * jax.random.normal(jax.random.fold_in(key, 23), noise_shape, jnp.float32)
    values = gain[..., None, None] * centre[None] + noise
    return jnp.clip(values, -12.0, 12.0).reshape(VISITS, DETS, SUBS, S_LOC, PIX).astype(jnp.bfloat16)


def draw_stamp_patch(key, part):
    count = SUBS * S_LOC
    share = jax.random.randint(jax.random.fold_in(key, 31), (PATCHES,), 1, 11)
    detector = jnp.arange(DETS)
    cover = jax.random.randint(jax.random.fold_in(key, 32), (DETS,), 1, 5)
    widest = jax.random.randint(jax.random.fold_in(key, 33), (), 0, DETS)
    cover = jnp.where(detector == widest, 4, cover)
    reach = jnp.arange(4)
    step_offset = jnp.mod(reach + 1, 4) - 1
    candidate = jnp.mod(detector[:, None] + step_offset[None, :], PATCHES)
    onehot = (candidate[:, :, None] == jnp.arange(PATCHES)[None, None, :]).astype(jnp.int32)
    usable = (reach[None, :] < cover[:, None]).astype(jnp.int32)
    cand_share = jnp.sum(onehot * share[None, None, :], axis=2) * usable
    bounds = jnp.cumsum(cand_share, axis=1)
    ticket = jax.random.randint(jax.random.fold_in(key, 34), (DETS, count), 0, 1 << 20)
    ticket = jnp.mod(ticket, bounds[:, 3:4])
    picked = jnp.sum((ticket[:, :, None] >= bounds[:, None, :]).astype(jnp.int32), axis=2)
    position = jnp.arange(count)
    first_slot = jax.random.randint(jax.random.fold_in(key, 35), (DETS,), 0, count)
    second_slot = jnp.mod(first_slot + jax.random.randint(jax.random.fold_in(key, 36), (DETS,), 1, count), count)
    picked = jnp.where(position[None, :] == first_slot[:, None], 0, picked)
    picked = jnp.where(position[None, :] == second_slot[:, None], cover[:, None] - 1, picked)
    chosen = jnp.take_along_axis(candidate, picked, axis=1)
    return chosen.astype(jnp.int32).reshape(DETS, SUBS, S_LOC)


def steps_of(stream_key, extent, split, smallest, top_value):
    def one(dim, parts):
        draws = jax.random.uniform(jax.random.fold_in(jax.random.fold_in(stream_key, 6), dim), (parts,), jnp.float32, smallest / len(split), top_value / len(split))
        return jnp.repeat(jnp.exp(draws), extent[dim] // parts).reshape((-1,) + (1,) * (len(extent) - dim - 1))

    loudness = one(*split[0])
    for cut in split[1:]:
        loudness = loudness * one(*cut)
    return loudness


def gaussian(key, shape, scale, most, kind=jnp.bfloat16):
    return jnp.clip(scale * jax.random.normal(key, shape, jnp.float32), -most, most).astype(kind)


def setup_inputs(seed: int = 0) -> dict:
    keys = jax.random.split(jax.random.key(seed), 7)
    return {
        "template": draw_template(jax.random.fold_in(keys[6], 71), 0),
        "science": draw_science(jax.random.fold_in(keys[6], 71), 0),
        "weight": jnp.clip(jnp.exp(math.log(2.0) - 1.3862944 * jax.random.uniform(keys[2], (VISITS, DETS, SUBS, S_LOC), jnp.float32) ** steps_of(keys[2], (VISITS, DETS, SUBS, S_LOC), ((0, 8), (1, 64)), -0.2, 0.2)), 0.5, 2.0).astype(jnp.bfloat16),
        "stamp_patch": draw_stamp_patch(jax.random.fold_in(keys[6], 71), 0),
        "basis_across": gaussian(keys[4], (NB, KS), 0.1, 0.6, jnp.float32),
        "basis_down": gaussian(keys[5], (NB, KS), 0.1, 0.6, jnp.float32),
    }


highest = lax.Precision.HIGHEST

def conv_tables(basis_across, basis_down, stamp_size):
    basis_count, taps = basis_across.shape
    template_size = stamp_size + taps - 1
    offset = jnp.arange(template_size)[:, None] - jnp.arange(stamp_size)[None, :]
    select = (offset[None, :, :] == jnp.arange(taps)[:, None, None]).astype(jnp.float32)
    across = basis_across.astype(jnp.bfloat16).astype(jnp.float32)
    downward = basis_down.astype(jnp.bfloat16).astype(jnp.float32)
    row_table = jnp.einsum('kj,jzx->zkx', across, select, precision=highest)
    row_table = row_table.reshape(template_size, basis_count * stamp_size).astype(jnp.bfloat16)
    col_table = jnp.einsum('kj,jzy->kyz', downward, select, precision=highest).astype(jnp.bfloat16)
    return (row_table, col_table)

def basis_images(stamps, row_table, col_table, stamp_size):
    stamp_count = stamps.shape[0]
    template_size = row_table.shape[0]
    basis_count = col_table.shape[0]
    across = jnp.dot(stamps.reshape(stamp_count * template_size, template_size).astype(jnp.float32), row_table.astype(jnp.float32), preferred_element_type=jnp.float32)
    across = lax.optimization_barrier(across.astype(jnp.bfloat16))
    across = across.reshape(stamp_count, template_size, basis_count, stamp_size).astype(jnp.float32)
    images = jnp.einsum('kyz,szkx->skyx', col_table.astype(jnp.float32), across, precision=highest)
    return images.astype(jnp.bfloat16).reshape(stamp_count, basis_count, stamp_size * stamp_size)

def solve_systems(matrices, rhs):
    factor = jnp.linalg.cholesky(matrices)
    inner = jax.scipy.linalg.solve_triangular(factor, rhs[..., None], lower=True)
    return jax.scipy.linalg.solve_triangular(factor, inner, lower=True, trans=1)[..., 0]

def reference(template, science, weight, stamp_patch, basis_across, basis_down):
    row_table, col_table = conv_tables(basis_across, basis_down, STAMP)
    stamps = template.reshape(STAMPS, TPIX)
    exposures = science.reshape(VISITS, STAMPS, PIX)
    weights = weight.reshape(VISITS, STAMPS).astype(jnp.float32)
    owners = stamp_patch.reshape(STAMPS)
    block_rows = math.gcd(STAMPS, 256)
    block_count = STAMPS // block_rows
    patch_ids = jnp.arange(PATCHES)

    def slices(block_index):
        first_row = block_index * block_rows
        stamp_rows = lax.dynamic_slice_in_dim(stamps, first_row, block_rows, 0)
        exposure_rows = lax.dynamic_slice_in_dim(exposures, first_row, block_rows, 1)
        weight_rows = lax.dynamic_slice_in_dim(weights, first_row, block_rows, 1)
        owner_rows = lax.dynamic_slice_in_dim(owners, first_row, block_rows, 0)
        member = (owner_rows[:, None] == patch_ids[None, :]).astype(jnp.float32)
        return (stamp_rows, exposure_rows, weight_rows, member)

    def accumulate(carry, block_index):
        matrices, rhs = carry
        stamp_rows, exposure_rows, weight_rows, member = slices(block_index)
        images = lax.optimization_barrier(basis_images(stamp_rows, row_table, col_table, STAMP))
        images = images.astype(jnp.float32)
        gram = jnp.einsum('skp,sjp->skj', images, images, precision=highest)
        project = jnp.einsum('vsp,skp->vsk', exposure_rows.astype(jnp.float32), images, precision=highest)
        weighted = weight_rows.T[:, :, None] * member[:, None, :]
        matrices = matrices + jnp.einsum('svq,skj->vqkj', weighted, gram, precision=highest)
        rhs = rhs + jnp.einsum('svq,vsk->vqk', weighted, project, precision=highest)
        return ((matrices, rhs), None)
    start_state = (jnp.zeros((VISITS, PATCHES, NB, NB), jnp.float32), jnp.zeros((VISITS, PATCHES, NB), jnp.float32))
    (matrices, rhs), unused = lax.scan(accumulate, start_state, jnp.arange(block_count))
    kernel_coef = solve_systems(matrices.reshape(VISITS * PATCHES, NB, NB), rhs.reshape(VISITS * PATCHES, NB)).reshape(VISITS, PATCHES, NB)

    def residual_block(block_index):
        stamp_rows, exposure_rows, weight_rows, member = slices(block_index)
        images = lax.optimization_barrier(basis_images(stamp_rows, row_table, col_table, STAMP))
        stamp_coef = jnp.einsum('sq,vqk->vsk', member, kernel_coef, precision=highest)
        stamp_coef = lax.optimization_barrier(stamp_coef.astype(jnp.bfloat16))
        model = jnp.einsum('vsk,skp->vsp', stamp_coef.astype(jnp.float32), images.astype(jnp.float32), precision=highest)
        diff = exposure_rows.astype(jnp.float32) - model
        return weight_rows * jnp.mean(diff * diff, axis=2)
    blocks = lax.map(residual_block, jnp.arange(block_count))
    residual = jnp.transpose(blocks, (1, 0, 2)).reshape(VISITS, DETS, SUBS, S_LOC)
    return (kernel_coef, residual)
```

```python
import functools

import jax
import jax.numpy as jnp
from jax import lax
from jax.experimental import pallas as pl
from jax.experimental.pallas import tpu as pltpu
from jax.sharding import PartitionSpec as P

MESH = pl.DeviceIdType.MESH
F32 = jnp.float32
BF16 = jnp.bfloat16

STAMP = 32
TAPS = 17
SIDE = 48
NB = 43
REACH = 4


def lanes(shape):
    return lax.broadcasted_iota(jnp.int32, shape, len(shape) - 1)


def tables(basis_across, basis_down):
    across = jnp.pad(basis_across.astype(BF16), ((0, 1), (0, 0)))
    down = jnp.pad(basis_down.astype(BF16), ((0, 5), (0, 0)))
    place = jnp.arange(SIDE)[:, None] - jnp.arange(128)[None, :] % STAMP
    row_table = jnp.zeros((SIDE, 44, 128), BF16)
    for tap in range(TAPS):
        row_table = jnp.where(
            (place == tap)[:, None, :], across[None, :, tap, None], row_table
        )
    place = jnp.arange(256)[None, :] % 32 - jnp.arange(16)[:, None]
    same = jnp.arange(8)[:, None] == jnp.arange(256)[None, :] // 32
    grouped = down.reshape(6, 8, TAPS)
    col_table = jnp.zeros((6, 16, 8, 256), BF16)
    for tap in range(TAPS):
        here = (place == tap)[None, :, None, :] & same[None, None, :, :]
        col_table = jnp.where(here, grouped[:, None, :, tap, None], col_table)
    return row_table.reshape(SIDE, 44 * 128), col_table.reshape(6 * 128, 256)


def inverse_4x4(m):
    p, q, s = m[0][0], m[0][1], m[1][1]
    i = 1.0 / (p * s - q * q)
    a, b, c = s * i, -q * i, p * i
    e, f, g, h = m[0][2], m[0][3], m[1][2], m[1][3]
    ae, af = a * e + b * g, a * f + b * h
    ce, cf = b * e + c * g, b * f + c * h
    t = m[2][2] - (e * ae + g * ce)
    u = m[2][3] - (e * af + g * cf)
    w = m[3][3] - (f * af + h * cf)
    j = 1.0 / (t * w - u * u)
    x, y, z = w * j, -u * j, t * j
    r00, r01 = -(ae * x + af * y), -(ae * y + af * z)
    r10, r11 = -(ce * x + cf * y), -(ce * y + cf * z)
    n00 = a - (r00 * ae + r01 * af)
    n01 = b - (r00 * ce + r01 * cf)
    n11 = c - (r10 * ce + r11 * cf)
    return (
        (n00, n01, r00, r01),
        (n01, n11, r10, r11),
        (r00, r10, x, y),
        (r01, r11, y, z),
    )


def solve(tiles):
    lane = lanes((8, 128))
    tiles = list(tiles)
    for block in range(11):
        first = 4 * block
        tile = tiles[first // 8]
        rows = [
            jnp.broadcast_to(tile[(first + c) % 8 : (first + c) % 8 + 1, :], (8, 128))
            for c in range(4)
        ]
        pivot = [[None] * 4 for _ in range(4)]
        for r in range(4):
            for c in range(r, 4):
                value = jnp.broadcast_to(rows[r][:, first + c : first + c + 1], (8, 128))
                pivot[r][c] = pivot[c][r] = value
        inverse = inverse_4x4(pivot)
        inside = (lane >= first) & (lane < first + 4)
        rows = [
            jnp.where(inside, jnp.where(lane == first + c, -1.0, 0.0), rows[c])
            for c in range(4)
        ]
        scaled = [
            (inverse[r][0] * rows[0] + inverse[r][1] * rows[1])
            + (inverse[r][2] * rows[2] + inverse[r][3] * rows[3])
            for r in range(4)
        ]
        for t in range((first + 4) // 8, 6):
            old = tiles[t]
            cols = [
                jnp.broadcast_to(old[:, first + c : first + c + 1], (8, 128))
                for c in range(4)
            ]
            change = (cols[0] * scaled[0] + cols[1] * scaled[1]) + (
                cols[2] * scaled[2] + cols[3] * scaled[3]
            )
            tiles[t] = jnp.where(inside, 0.0, old) - change
    return tiles[5][7:8, :]


def unpack(low, high):
    lane = lanes((8, 128))
    row = lax.broadcasted_iota(jnp.int32, (8, 128), 0)
    tiles = [low, high]
    tiles += [pltpu.roll(x, 96, 1) for x in (low, high)]
    tiles += [pltpu.roll(x, 80, 1) for x in (low, high)]
    full = jnp.concatenate(tiles, axis=0)
    keep = lanes((SIDE, 128)) // 16 >= lax.broadcasted_iota(jnp.int32, (SIDE, 128), 0) // 16
    upper = jnp.where(keep & (lanes((SIDE, 128)) < SIDE), full, 0.0)
    square = jnp.concatenate([upper, jnp.zeros((128 - SIDE, 128), F32)], axis=0)
    flipped = square.T[:SIDE]
    full = jnp.where(keep, upper, flipped)
    tiles = [full[8 * t : 8 * t + 8] for t in range(6)]
    right = jnp.where(
        lane < 32,
        jnp.broadcast_to(pltpu.roll(low, 32, 1)[0:1], (8, 128)),
        jnp.broadcast_to(pltpu.roll(low, 64, 1)[1:2], (8, 128)),
    )
    right = jnp.where(lane < NB, right, 0.0)
    tiles[5] = jnp.where(row == 7, right, tiles[5])
    tiles[5] = jnp.where((row == 3) & (lane == NB), 1.0, tiles[5])
    return tiles


def kernel(
    visits,
    patches,
    stamps_ref,
    row_ref,
    col_ref,
    weight_ref,
    offset_ref,
    offset_smem,
    science_ref,
    coef_ref,
    residual_ref,
    rows_scr,
    wide_scr,
    image_scr,
    sci_recv,
    sci_scr,
    w_recv,
    gram_scr,
    proj_scr,
    msg,
    inbox,
    coef_row,
    coef_box,
    own_sem,
    sci_send,
    sci_sem,
    w_send,
    w_sem,
    msg_send,
    msg_sem,
    coef_send,
    coef_sem,
):
    me_v = lax.axis_index("visit")
    me_q = lax.axis_index("patch")
    barrier = pltpu.get_barrier_semaphore()
    span = 2 * REACH - 3

    def peer(step):
        v = lax.rem(me_v + lax.rem(step, visits), visits)
        q = lax.rem(me_q + lax.div(step, visits) - 2 + patches, patches)
        return v, q

    @pl.loop(0, span * visits)
    def greet(step):
        @pl.when(step != 2 * visits)
        def _():
            v, q = peer(step)
            pl.semaphore_signal(barrier, inc=1, device_id=(v, q), device_id_type=MESH)

    own_copy = pltpu.make_async_copy(science_ref.at[me_v], sci_recv.at[me_v], own_sem)
    own_copy.start()
    w_recv[pl.ds(me_v, 1), :] = weight_ref[pl.ds(me_v, 1), :]

    pl.semaphore_wait(barrier, span * visits - 1)

    @pl.loop(1, visits)
    def send_science(step):
        v = lax.rem(me_v + step, visits)
        pltpu.make_async_remote_copy(
            src_ref=weight_ref.at[pl.ds(v, 1), :],
            dst_ref=w_recv.at[pl.ds(me_v, 1), :],
            send_sem=w_send,
            recv_sem=w_sem,
            device_id=(v, me_q),
            device_id_type=MESH,
        ).start()
        pltpu.make_async_remote_copy(
            src_ref=science_ref.at[v],
            dst_ref=sci_recv.at[me_v],
            send_sem=sci_send,
            recv_sem=sci_sem,
            device_id=(v, me_q),
            device_id_type=MESH,
        ).start()

    quarter = lax.broadcasted_iota(jnp.int32, (SIDE, 256), 1) % 128 // STAMP
    masks = [(quarter == s).astype(F32).astype(BF16) for s in range(4)]
    stamps = stamps_ref[...]
    rows_scr[44:48] = jnp.zeros((4, SIDE, 512), BF16)

    @pl.loop(0, 22)
    def make_rows(pair):
        table = row_ref[:, pl.ds(pl.multiple_of(pair * 256, 256), 256)]
        right = jnp.concatenate([table * m for m in masks], axis=0)
        out = jnp.dot(stamps, right, preferred_element_type=F32).astype(BF16)
        for j in range(2):
            for g in range(4):
                rows_scr[2 * pair + j, :, 128 * g : 128 * g + 128] = out[
                    SIDE * g : SIDE * g + SIDE, 128 * j : 128 * j + 128
                ]

    @pl.loop(0, 6)
    def make_images(group):
        first = pl.multiple_of(group * 8, 8)
        left = col_ref[pl.ds(pl.multiple_of(group * 128, 128), 128), :]
        for half in range(2):
            right = rows_scr[pl.ds(first, 8), 16 * half : 16 * half + 32, :]
            out = jnp.dot(left, right.reshape(256, 512), preferred_element_type=F32)
            wide_scr[16 * half : 16 * half + 16, pl.ds(first, 8), :] = out.reshape(16, 8, 512)

    lane = lanes((SIDE, 128))
    even = lane // STAMP % 2 == 0
    lower = lane < 64

    @pl.loop(0, 8)
    def regroup(quad):
        for g in range(4):
            part = [
                wide_scr[4 * quad + r, :, 128 * g : 128 * g + 128] for r in range(4)
            ]
            for a, b in ((0, 1), (2, 3)):
                x, y = part[a], part[b]
                part[a] = jnp.where(even, x, pltpu.roll(y, 32, 1))
                part[b] = jnp.where(even, pltpu.roll(x, 96, 1), y)
            for a, b in ((0, 2), (1, 3)):
                x, y = part[a], part[b]
                part[a] = jnp.where(lower, x, pltpu.roll(y, 64, 1))
                part[b] = jnp.where(lower, pltpu.roll(x, 64, 1), y)
            for s in range(4):
                image_scr[4 * g + s, :, pl.ds(pl.multiple_of(quad * 128, 128), 128)] = part[
                    s
                ].astype(BF16)

    own_copy.wait()
    pltpu.make_async_copy(sci_recv.at[1:], sci_recv.at[1:], sci_sem).wait()
    pltpu.make_async_copy(w_recv.at[1:], w_recv.at[1:], w_sem).wait()

    for v in range(8):
        for t in range(8):
            sci_scr[128 * t + 16 * v : 128 * t + 16 * v + 16, :] = sci_recv[
                v, :, 128 * t : 128 * t + 128
            ].astype(F32)

    def exposures(s):
        return [sci_scr[pl.ds(128 * t + s, 8, stride=16), :] for t in range(8)]

    nothing = jnp.zeros((8, 1024), F32)
    lane16 = lanes((16, 128))

    @pl.loop(0, 16)
    def make_grams(s):
        image = image_scr[s]
        science = jnp.concatenate(exposures(s), axis=1)
        left = jnp.concatenate(
            [image, jnp.concatenate([science, nothing], axis=0).astype(BF16)], axis=0
        )
        out = lax.dot_general(
            left, image, (((1,), (1,)), ((), ())), preferred_element_type=F32
        )
        out = jnp.concatenate([out, jnp.zeros((64, 80), F32)], axis=1)
        packed = jnp.where(
            lane16 < 48,
            out[0:16],
            jnp.where(
                lane16 < 80,
                pltpu.roll(out[16:32], 32, 1),
                pltpu.roll(out[32:48], 48, 1),
            ),
        )
        gram_scr[pl.ds(pl.multiple_of(s * 16, 16), 16), :] = packed
        proj_scr[pl.ds(pl.multiple_of(s * 8, 8), 8), :] = out[48:56]

    weights = w_recv[...]
    offset = jnp.broadcast_to(offset_ref[...], (8, 128))
    weighted = jnp.concatenate(
        [jnp.where(offset == o, weights, 0.0) for o in range(REACH)], axis=0
    )
    left = weighted[:, :16].astype(BF16)
    left = jnp.concatenate([left] * 3, axis=1)
    right = jnp.concatenate(
        [gram_scr[pl.ds(r, 16, stride=16), :] for r in range(16)], axis=1
    )
    top = right.astype(BF16)
    rest = right - top.astype(F32)
    middle = rest.astype(BF16)
    low = (rest - middle.astype(F32)).astype(BF16)
    systems = jnp.dot(
        left, jnp.concatenate([top, middle, low], axis=0), preferred_element_type=F32
    )
    sides = [jnp.zeros((8, 128), F32) for _ in range(REACH)]
    for s in range(16):
        for o in range(REACH):
            factor = jnp.broadcast_to(weighted[8 * o : 8 * o + 8, s : s + 1], (8, 128))
            sides[o] = sides[o] + factor * proj_scr[8 * s : 8 * s + 8, :]
    side = jnp.concatenate(sides, axis=0)
    lane32 = lanes((32, 128))
    for r in range(16):
        tile = systems[:, 128 * r : 128 * r + 128]
        if r == 0:
            tile = jnp.where(lane32 >= 96, pltpu.roll(side, 96, 1), tile)
        if r == 1:
            tile = jnp.where(lane32 >= 96, pltpu.roll(side, 64, 1), tile)
        msg[pl.ds(r, 32, stride=16), :] = tile

    home = visits + me_v

    def slot(n):
        return pl.ds(pl.multiple_of(n * 16, 16), 16)

    @pl.loop(0, REACH * visits)
    def send_systems(step):
        o = REACH - 1 - lax.div(step, visits)
        v = lax.rem(me_v + lax.rem(step, visits), visits)

        @pl.when(o * visits + v != home)
        def _():
            pltpu.make_async_remote_copy(
                src_ref=msg.at[slot(o * visits + v), :],
                dst_ref=inbox.at[slot(o * visits + me_v), :],
                send_sem=msg_send,
                recv_sem=msg_sem,
                device_id=(v, lax.rem(me_q + o - 1 + patches, patches)),
                device_id_type=MESH,
            ).start()

    inbox[slot(home), :] = msg[slot(home), :]
    pltpu.make_async_copy(inbox.at[16:], inbox.at[16:], msg_sem).wait()
    total = inbox[0:16, :]
    for n in range(1, REACH * 8):
        total = total + inbox[16 * n : 16 * n + 16, :]

    answer = solve(unpack(total[0:8], total[8:16]))
    answer = jnp.where(lanes((1, 128)) < NB, answer, 0.0)
    coef_row[...] = answer
    coef_box[1, pl.ds(me_v, 1), :] = answer

    @pl.loop(0, REACH * visits)
    def send_coefs(step):
        o = lax.div(step, visits)
        v = lax.rem(me_v + lax.rem(step, visits), visits)

        @pl.when(o * visits + v != home)
        def _():
            pltpu.make_async_remote_copy(
                src_ref=coef_row,
                dst_ref=coef_box.at[o, pl.ds(me_v, 1), :],
                send_sem=coef_send,
                recv_sem=coef_sem,
                device_id=(v, lax.rem(me_q - o + 1 + patches, patches)),
                device_id_type=MESH,
            ).start()

    coef_ref[0] = answer[:, :NB]
    pltpu.make_async_copy(inbox.at[0:31], inbox.at[0:31], coef_sem).wait()

    lane8 = lanes((8, 128))

    def fit(s, held):
        choice = offset_smem[0, s]
        coefs = coef_box[choice]
        model = jnp.dot(
            coefs[:, :SIDE].astype(BF16), image_scr[s], preferred_element_type=F32
        )
        diff = jnp.concatenate(exposures(s), axis=1) - model
        square = diff * diff
        part = square[:, 0:128]
        for t in range(1, 8):
            part = part + square[:, 128 * t : 128 * t + 128]
        return jnp.where(lane8 == s, jnp.sum(part, axis=1, keepdims=True), held)

    held = lax.fori_loop(0, 16, fit, jnp.zeros((8, 128), F32))
    held = held * weights * (1.0 / 1024.0)
    for v in range(8):
        residual_ref[v, 0] = held[v : v + 1, :16]

    pltpu.make_async_copy(sci_recv.at[1:], sci_recv.at[1:], sci_send).wait()
    pltpu.make_async_copy(w_recv.at[1:], w_recv.at[1:], w_send).wait()
    pltpu.make_async_copy(inbox.at[16:], inbox.at[16:], msg_send).wait()
    pltpu.make_async_copy(inbox.at[0:31], inbox.at[0:31], coef_send).wait()


def on_device(template, science, weight, stamp_patch, basis_across, basis_down):
    visits = lax.axis_size("visit")
    patches = lax.axis_size("patch")
    row_table, col_table = tables(basis_across, basis_down)
    stamps = template.reshape(4, 4, SIDE, SIDE).transpose(0, 2, 1, 3).reshape(192, 192)
    weights = jnp.pad(weight.reshape(8, 16).astype(F32), ((0, 0), (0, 112)))
    offset = jnp.mod(stamp_patch.reshape(1, 16) - lax.axis_index("patch") + 1, patches)
    offset_row = jnp.pad(offset, ((0, 0), (0, 112)))
    vmem = pl.BlockSpec(memory_space=pltpu.VMEM)
    dma = pltpu.SemaphoreType.DMA
    return pl.pallas_call(
        functools.partial(kernel, visits, patches),
        out_shape=(
            jax.ShapeDtypeStruct((1, 1, NB), F32),
            jax.ShapeDtypeStruct((8, 1, 1, 16), F32),
        ),
        in_specs=[vmem] * 5
        + [pl.BlockSpec(memory_space=pltpu.SMEM), pl.BlockSpec(memory_space=pl.ANY)],
        out_specs=(vmem, vmem),
        scratch_shapes=[
            pltpu.VMEM((48, SIDE, 512), BF16),
            pltpu.VMEM((STAMP, SIDE, 512), F32),
            pltpu.VMEM((16, SIDE, 1024), BF16),
            pltpu.VMEM((8, 16, 1024), BF16),
            pltpu.VMEM((1024, 128), F32),
            pltpu.VMEM((8, 128), F32),
            pltpu.VMEM((256, 128), F32),
            pltpu.VMEM((128, 128), F32),
            pltpu.VMEM((512, 128), F32),
            pltpu.VMEM((512, 128), F32),
            pltpu.VMEM((1, 128), F32),
            pltpu.VMEM((REACH, 8, 128), F32),
        ]
        + [dma] * 9,
        compiler_params=pltpu.CompilerParams(
            collective_id=0, has_side_effects=True, vmem_limit_bytes=32 * 1024 * 1024
        ),
    )(stamps, row_table, col_table, weights, offset_row, offset, science.reshape(8, 16, 1024))


def solution(mesh):
    return jax.shard_map(
        on_device,
        mesh=mesh,
        in_specs=(
            P("patch", "visit", None, None),
            P("visit", "patch", None, None, None),
            P("visit", "patch", None, None),
            P("patch", "visit", None),
            P(),
            P(),
        ),
        out_specs=(P("visit", "patch", None), P(None, "patch", "visit", None)),
        check_vma=False,
    )
```

```python
import functools

import jax
import jax.numpy as jnp
from jax import lax
from jax.experimental import pallas as pl
from jax.experimental.pallas import tpu as pltpu
from jax.sharding import PartitionSpec as P

MESH = pl.DeviceIdType.MESH
F32 = jnp.float32
BF16 = jnp.bfloat16

STAMP = 32
TAPS = 17
SIDE = 48
NB = 43
REACH = 4


def lanes(shape):
    return lax.broadcasted_iota(jnp.int32, shape, len(shape) - 1)


def inverse_4x4(m):
    p, q, s = m[0][0], m[0][1], m[1][1]
    i = 1.0 / (p * s - q * q)
    a, b, c = s * i, -q * i, p * i
    e, f, g, h = m[0][2], m[0][3], m[1][2], m[1][3]
    ae, af = a * e + b * g, a * f + b * h
    ce, cf = b * e + c * g, b * f + c * h
    t = m[2][2] - (e * ae + g * ce)
    u = m[2][3] - (e * af + g * cf)
    w = m[3][3] - (f * af + h * cf)
    j = 1.0 / (t * w - u * u)
    x, y, z = w * j, -u * j, t * j
    r00, r01 = -(ae * x + af * y), -(ae * y + af * z)
    r10, r11 = -(ce * x + cf * y), -(ce * y + cf * z)
    n00 = a - (r00 * ae + r01 * af)
    n01 = b - (r00 * ce + r01 * cf)
    n11 = c - (r10 * ce + r11 * cf)
    return (
        (n00, n01, r00, r01),
        (n01, n11, r10, r11),
        (r00, r10, x, y),
        (r01, r11, y, z),
    )


def solve(tiles):
    lane = lanes((8, 128))
    tiles = list(tiles)
    for block in range(11):
        first = 4 * block
        tile = tiles[first // 8]
        rows = [
            jnp.broadcast_to(tile[(first + c) % 8 : (first + c) % 8 + 1, :], (8, 128))
            for c in range(4)
        ]
        pivot = [[None] * 4 for _ in range(4)]
        for r in range(4):
            for c in range(r, 4):
                value = jnp.broadcast_to(rows[r][:, first + c : first + c + 1], (8, 128))
                pivot[r][c] = pivot[c][r] = value
        inverse = inverse_4x4(pivot)
        inside = (lane >= first) & (lane < first + 4)
        rows = [
            jnp.where(inside, jnp.where(lane == first + c, -1.0, 0.0), rows[c])
            for c in range(4)
        ]
        scaled = [
            (inverse[r][0] * rows[0] + inverse[r][1] * rows[1])
            + (inverse[r][2] * rows[2] + inverse[r][3] * rows[3])
            for r in range(4)
        ]
        for t in range((first + 4) // 8, 6):
            old = tiles[t]
            cols = [
                jnp.broadcast_to(old[:, first + c : first + c + 1], (8, 128))
                for c in range(4)
            ]
            change = (cols[0] * scaled[0] + cols[1] * scaled[1]) + (
                cols[2] * scaled[2] + cols[3] * scaled[3]
            )
            tiles[t] = jnp.where(inside, 0.0, old) - change
    return tiles[5][7:8, :]


def unpack(low, high):
    lane = lanes((8, 128))
    row = lax.broadcasted_iota(jnp.int32, (8, 128), 0)
    tiles = [low, high]
    tiles += [pltpu.roll(x, 96, 1) for x in (low, high)]
    tiles += [pltpu.roll(x, 80, 1) for x in (low, high)]
    full = jnp.concatenate(tiles, axis=0)
    keep = lanes((SIDE, 128)) // 16 >= lax.broadcasted_iota(jnp.int32, (SIDE, 128), 0) // 16
    upper = jnp.where(keep & (lanes((SIDE, 128)) < SIDE), full, 0.0)
    square = jnp.concatenate([upper, jnp.zeros((128 - SIDE, 128), F32)], axis=0)
    flipped = square.T[:SIDE]
    full = jnp.where(keep, upper, flipped)
    tiles = [full[8 * t : 8 * t + 8] for t in range(6)]
    right = jnp.where(
        lane < 32,
        jnp.broadcast_to(pltpu.roll(low, 32, 1)[0:1], (8, 128)),
        jnp.broadcast_to(pltpu.roll(low, 64, 1)[1:2], (8, 128)),
    )
    right = jnp.where(lane < NB, right, 0.0)
    tiles[5] = jnp.where(row == 7, right, tiles[5])
    tiles[5] = jnp.where((row == 3) & (lane == NB), 1.0, tiles[5])
    return tiles


def kernel(
    visits,
    patches,
    template_ref,
    across_ref,
    down_ref,
    weight_ref,
    patch_ref,
    science_ref,
    coef_ref,
    residual_ref,
    template_own,
    across_own,
    down_own,
    weight_own,
    patch_own,
    across_scr,
    down_scr,
    turn_scr,
    choice_scr,
    w_own,
    rows_scr,
    wide_scr,
    image_scr,
    sci_recv,
    sci_scr,
    w_recv,
    gram_scr,
    proj_scr,
    msg,
    inbox,
    coef_row,
    coef_box,
    own_sem,
    small_sem,
    sci_send,
    sci_sem,
    w_send,
    w_sem,
    msg_send,
    msg_sem,
    coef_send,
    coef_sem,
):
    me_v = lax.axis_index("visit")
    me_q = lax.axis_index("patch")
    barrier = pltpu.get_barrier_semaphore()
    span = 2 * REACH - 3

    def peer(step):
        v = lax.rem(me_v + lax.rem(step, visits), visits)
        q = lax.rem(me_q + lax.div(step, visits) - 2 + patches, patches)
        return v, q

    small = [
        pltpu.make_async_copy(source, target, small_sem.at[n])
        for n, (source, target) in enumerate(
            (
                (weight_ref, weight_own),
                (across_ref, across_own),
                (down_ref, down_own),
                (patch_ref, patch_own),
                (template_ref, template_own),
            )
        )
    ]
    for copy in small:
        copy.start()

    @pl.loop(0, span * visits)
    def greet(step):
        @pl.when(step != 2 * visits)
        def _():
            v, q = peer(step)
            pl.semaphore_signal(barrier, inc=1, device_id=(v, q), device_id_type=MESH)

    own_copy = pltpu.make_async_copy(science_ref.at[0, 0, me_v], sci_recv.at[me_v], own_sem)
    own_copy.start()
    for copy in small:
        copy.wait()
    w_own[...] = jnp.concatenate(
        [weight_own[0, 0].astype(F32), jnp.zeros((8, 112), F32)], axis=1
    )
    w_recv[pl.ds(me_v, 1), :] = w_own[pl.ds(me_v, 1), :]
    tap = lax.broadcasted_iota(jnp.int32, (TAPS, 128), 0)
    column = lanes((TAPS, 128)) % STAMP
    backwards = ((column + tap) % STAMP == 0).astype(F32).astype(BF16)
    forwards = (column == tap).astype(F32).astype(BF16)
    nothing5 = jnp.zeros((5, 128), F32)
    across_scr[NB:, :] = nothing5
    first_axes = (((0,), (0,)), ((), ()))
    across_scr[0:NB, :] = lax.dot_general(
        across_own[...].astype(BF16), backwards, first_axes, preferred_element_type=F32
    )
    down_scr[NB:, :] = nothing5
    down_scr[0:NB, :] = lax.dot_general(
        down_own[...].astype(BF16), forwards, first_axes, preferred_element_type=F32
    )
    near = jnp.concatenate([patch_own[0], jnp.zeros((1, 112), jnp.int32)], axis=1)
    near = lax.rem(near - me_q + 1 + patches, patches).astype(F32)
    near16 = jnp.broadcast_to(near, (16, 128))
    diagonal = lanes((16, 128)) == lax.broadcasted_iota(jnp.int32, (16, 128), 0)
    choice_scr[...] = jnp.broadcast_to(
        jnp.sum(jnp.where(diagonal, near16, 0.0), axis=1, keepdims=True), (16, 128)
    )
    flat = template_own[0, 0].astype(F32)
    for z in range(SIDE):
        turn_scr[16 * z : 16 * z + 16, 0:SIDE] = flat[:, SIDE * z : SIDE * z + SIDE]
    stamps = jnp.concatenate(
        [
            jnp.concatenate(
                [
                    turn_scr[pl.ds(4 * g + s, SIDE, stride=16), :][:, :SIDE]
                    for s in range(4)
                ],
                axis=1,
            )
            for g in range(4)
        ],
        axis=0,
    ).astype(BF16)
    pl.semaphore_wait(barrier, span * visits - 1)

    @pl.loop(1, visits)
    def send_science(step):
        v = lax.rem(me_v + step, visits)
        pltpu.make_async_remote_copy(
            src_ref=w_own.at[pl.ds(v, 1), :],
            dst_ref=w_recv.at[pl.ds(me_v, 1), :],
            send_sem=w_send,
            recv_sem=w_sem,
            device_id=(v, me_q),
            device_id_type=MESH,
        ).start()
        pltpu.make_async_remote_copy(
            src_ref=science_ref.at[0, 0, v],
            dst_ref=sci_recv.at[me_v],
            send_sem=sci_send,
            recv_sem=sci_sem,
            device_id=(v, me_q),
            device_id_type=MESH,
        ).start()

    shape = (SIDE, 128)
    past = lax.broadcasted_iota(jnp.int32, shape, 0) - lanes(shape) % STAMP
    band = (past >= 0) & (past < TAPS)
    masks = [
        (band & (lanes(shape) // STAMP == s)).astype(F32).astype(BF16) for s in range(4)
    ]
    rows_scr[44:48] = jnp.zeros((4, SIDE, 512), BF16)

    @pl.loop(0, 22)
    def make_rows(pair):
        right = []
        for j in range(2):
            taps = across_scr[pl.ds(2 * pair + j, 1), :]
            table = pltpu.roll(
                jnp.broadcast_to(taps, (STAMP, 128)), 0, 1, stride=1, stride_axis=0
            )
            table = jnp.concatenate([table, table[: SIDE - STAMP]], axis=0).astype(BF16)
            right.append(jnp.concatenate([table * m for m in masks], axis=0))
        right = jnp.concatenate(right, axis=1)
        out = jnp.dot(stamps, right, preferred_element_type=F32).astype(BF16)
        for j in range(2):
            for g in range(4):
                rows_scr[2 * pair + j, :, 128 * g : 128 * g + 128] = out[
                    SIDE * g : SIDE * g + SIDE, 128 * j : 128 * j + 128
                ]

    within = lanes((8, 128)) // STAMP - lax.broadcasted_iota(jnp.int32, (8, 128), 0)
    owner, owner4 = within == 0, within == -4

    @pl.loop(0, 6)
    def make_images(group):
        first = pl.multiple_of(group * 8, 8)
        taps = down_scr[pl.ds(first, 8), :]
        left = jnp.concatenate(
            [jnp.where(owner, taps, 0.0), jnp.where(owner4, taps, 0.0)], axis=1
        )
        left = jnp.concatenate(
            [left]
            + [
                jnp.concatenate(
                    [
                        pltpu.roll(left[:, :128], y, 1),
                        pltpu.roll(left[:, 128:], y, 1),
                    ],
                    axis=1,
                )
                for y in range(1, 16)
            ],
            axis=0,
        ).astype(BF16)
        for half in range(2):
            right = rows_scr[pl.ds(first, 8), 16 * half : 16 * half + 32, :]
            out = jnp.dot(left, right.reshape(256, 512), preferred_element_type=F32)
            wide_scr[16 * half : 16 * half + 16, pl.ds(first, 8), :] = out.reshape(16, 8, 512)

    lane = lanes((SIDE, 128))
    even = lane // STAMP % 2 == 0
    lower = lane < 64

    @pl.loop(0, 8)
    def regroup(quad):
        for g in range(4):
            part = [
                wide_scr[4 * quad + r, :, 128 * g : 128 * g + 128] for r in range(4)
            ]
            for a, b in ((0, 1), (2, 3)):
                x, y = part[a], part[b]
                part[a] = jnp.where(even, x, pltpu.roll(y, 32, 1))
                part[b] = jnp.where(even, pltpu.roll(x, 96, 1), y)
            for a, b in ((0, 2), (1, 3)):
                x, y = part[a], part[b]
                part[a] = jnp.where(lower, x, pltpu.roll(y, 64, 1))
                part[b] = jnp.where(lower, pltpu.roll(x, 64, 1), y)
            for s in range(4):
                image_scr[4 * g + s, :, pl.ds(pl.multiple_of(quad * 128, 128), 128)] = part[
                    s
                ].astype(BF16)

    own_copy.wait()
    pltpu.make_async_copy(sci_recv.at[1:], sci_recv.at[1:], sci_sem).wait()
    pltpu.make_async_copy(w_recv.at[1:], w_recv.at[1:], w_sem).wait()

    for v in range(8):
        for t in range(8):
            sci_scr[128 * t + 16 * v : 128 * t + 16 * v + 16, :] = sci_recv[
                v, :, 128 * t : 128 * t + 128
            ].astype(F32)

    def exposures(s):
        return [sci_scr[pl.ds(128 * t + s, 8, stride=16), :] for t in range(8)]

    nothing = jnp.zeros((8, 1024), F32)
    lane16 = lanes((16, 128))

    @pl.loop(0, 16)
    def make_grams(s):
        image = image_scr[s]
        science = jnp.concatenate(exposures(s), axis=1)
        left = jnp.concatenate(
            [image, jnp.concatenate([science, nothing], axis=0).astype(BF16)], axis=0
        )
        out = lax.dot_general(
            left, image, (((1,), (1,)), ((), ())), preferred_element_type=F32
        )
        out = jnp.concatenate([out, jnp.zeros((64, 80), F32)], axis=1)
        packed = jnp.where(
            lane16 < 48,
            out[0:16],
            jnp.where(
                lane16 < 80,
                pltpu.roll(out[16:32], 32, 1),
                pltpu.roll(out[32:48], 48, 1),
            ),
        )
        gram_scr[pl.ds(pl.multiple_of(s * 16, 16), 16), :] = packed
        proj_scr[pl.ds(pl.multiple_of(s * 8, 8), 8), :] = out[48:56]

    weights = w_recv[...]
    offset = near16[0:8]
    weighted = jnp.concatenate(
        [jnp.where(offset == float(o), weights, 0.0) for o in range(REACH)], axis=0
    )
    left = weighted[:, :16].astype(BF16)
    left = jnp.concatenate([left] * 3, axis=1)
    right = jnp.concatenate(
        [gram_scr[pl.ds(r, 16, stride=16), :] for r in range(16)], axis=1
    )
    top = right.astype(BF16)
    rest = right - top.astype(F32)
    middle = rest.astype(BF16)
    low = (rest - middle.astype(F32)).astype(BF16)
    systems = jnp.dot(
        left, jnp.concatenate([top, middle, low], axis=0), preferred_element_type=F32
    )
    sides = [jnp.zeros((8, 128), F32) for _ in range(REACH)]
    for s in range(16):
        for o in range(REACH):
            factor = jnp.broadcast_to(weighted[8 * o : 8 * o + 8, s : s + 1], (8, 128))
            sides[o] = sides[o] + factor * proj_scr[8 * s : 8 * s + 8, :]
    side = jnp.concatenate(sides, axis=0)
    lane32 = lanes((32, 128))
    for r in range(16):
        tile = systems[:, 128 * r : 128 * r + 128]
        if r == 0:
            tile = jnp.where(lane32 >= 96, pltpu.roll(side, 96, 1), tile)
        if r == 1:
            tile = jnp.where(lane32 >= 96, pltpu.roll(side, 64, 1), tile)
        msg[pl.ds(r, 32, stride=16), :] = tile

    home = visits + me_v

    def slot(n):
        return pl.ds(pl.multiple_of(n * 16, 16), 16)

    @pl.loop(0, REACH * visits)
    def send_systems(step):
        o = REACH - 1 - lax.div(step, visits)
        v = lax.rem(me_v + lax.rem(step, visits), visits)

        @pl.when(o * visits + v != home)
        def _():
            pltpu.make_async_remote_copy(
                src_ref=msg.at[slot(o * visits + v), :],
                dst_ref=inbox.at[slot(o * visits + me_v), :],
                send_sem=msg_send,
                recv_sem=msg_sem,
                device_id=(v, lax.rem(me_q + o - 1 + patches, patches)),
                device_id_type=MESH,
            ).start()

    inbox[slot(home), :] = msg[slot(home), :]
    pltpu.make_async_copy(inbox.at[16:], inbox.at[16:], msg_sem).wait()
    total = inbox[0:16, :]
    for n in range(1, REACH * 8):
        total = total + inbox[16 * n : 16 * n + 16, :]

    answer = solve(unpack(total[0:8], total[8:16]))
    answer = jnp.where(lanes((1, 128)) < NB, answer, 0.0)
    coef_row[...] = answer
    coef_box[1, pl.ds(me_v, 1), :] = answer

    @pl.loop(0, REACH * visits)
    def send_coefs(step):
        o = lax.div(step, visits)
        v = lax.rem(me_v + lax.rem(step, visits), visits)

        @pl.when(o * visits + v != home)
        def _():
            pltpu.make_async_remote_copy(
                src_ref=coef_row,
                dst_ref=coef_box.at[o, pl.ds(me_v, 1), :],
                send_sem=coef_send,
                recv_sem=coef_sem,
                device_id=(v, lax.rem(me_q - o + 1 + patches, patches)),
                device_id_type=MESH,
            ).start()

    coef_ref[0] = answer[:, :NB]
    pltpu.make_async_copy(inbox.at[0:31], inbox.at[0:31], coef_sem).wait()

    lane8 = lanes((8, 128))

    def fit(s, held):
        choice = jnp.broadcast_to(choice_scr[pl.ds(s, 1), :], (8, 128))
        coefs = coef_box[0]
        for o in range(1, REACH):
            coefs = jnp.where(choice == float(o), coef_box[o], coefs)
        model = jnp.dot(
            coefs[:, :SIDE].astype(BF16), image_scr[s], preferred_element_type=F32
        )
        diff = jnp.concatenate(exposures(s), axis=1) - model
        square = diff * diff
        part = square[:, 0:128]
        for t in range(1, 8):
            part = part + square[:, 128 * t : 128 * t + 128]
        return jnp.where(lane8 == s, jnp.sum(part, axis=1, keepdims=True), held)

    held = lax.fori_loop(0, 16, fit, jnp.zeros((8, 128), F32))
    held = held * weights * (1.0 / 1024.0)
    for v in range(8):
        residual_ref[v, 0] = held[v : v + 1, :16]

    pltpu.make_async_copy(sci_recv.at[1:], sci_recv.at[1:], sci_send).wait()
    pltpu.make_async_copy(w_recv.at[1:], w_recv.at[1:], w_send).wait()
    pltpu.make_async_copy(inbox.at[16:], inbox.at[16:], msg_send).wait()
    pltpu.make_async_copy(inbox.at[0:31], inbox.at[0:31], coef_send).wait()


def on_device(template, science, weight, stamp_patch, basis_across, basis_down):
    visits = lax.axis_size("visit")
    patches = lax.axis_size("patch")
    vmem = pl.BlockSpec(memory_space=pltpu.VMEM)
    dma = pltpu.SemaphoreType.DMA
    return pl.pallas_call(
        functools.partial(kernel, visits, patches),
        out_shape=(
            jax.ShapeDtypeStruct((1, 1, NB), F32),
            jax.ShapeDtypeStruct((8, 1, 1, 16), F32),
        ),
        in_specs=[pl.BlockSpec(memory_space=pltpu.HBM)] * 6,
        out_specs=(vmem, vmem),
        scratch_shapes=[
            pltpu.VMEM(template.shape, BF16),
            pltpu.VMEM((TAPS, NB), F32),
            pltpu.VMEM((TAPS, NB), F32),
            pltpu.VMEM(weight.shape, BF16),
            pltpu.VMEM(stamp_patch.shape, jnp.int32),
            pltpu.VMEM((SIDE, 128), F32),
            pltpu.VMEM((SIDE, 128), F32),
            pltpu.VMEM((SIDE * 16, 128), F32),
            pltpu.VMEM((16, 128), F32),
            pltpu.VMEM((8, 128), F32),
            pltpu.VMEM((48, SIDE, 512), BF16),
            pltpu.VMEM((STAMP, SIDE, 512), F32),
            pltpu.VMEM((16, SIDE, 1024), BF16),
            pltpu.VMEM((8, 16, 1024), BF16),
            pltpu.VMEM((1024, 128), F32),
            pltpu.VMEM((8, 128), F32),
            pltpu.VMEM((256, 128), F32),
            pltpu.VMEM((128, 128), F32),
            pltpu.VMEM((512, 128), F32),
            pltpu.VMEM((512, 128), F32),
            pltpu.VMEM((1, 128), F32),
            pltpu.VMEM((REACH, 8, 128), F32),
        ]
        + [dma, dma((5,))] + [dma] * 8,
        compiler_params=pltpu.CompilerParams(
            collective_id=0, has_side_effects=True, vmem_limit_bytes=60 * 1024 * 1024
        ),
    )(template, basis_across.T, basis_down.T, weight, stamp_patch, science)


def solution(mesh):
    return jax.shard_map(
        on_device,
        mesh=mesh,
        in_specs=(
            P("patch", "visit", None, None),
            P("visit", "patch", None, None, None),
            P("visit", "patch", None, None),
            P("patch", "visit", None),
            P(),
            P(),
        ),
        out_specs=(P("visit", "patch", None), P(None, "patch", "visit", None)),
        check_vma=False,
    )
```

```python
import functools

import jax
import jax.numpy as jnp
from jax import lax
from jax.experimental import pallas as pl
from jax.experimental.pallas import tpu as pltpu
from jax.sharding import PartitionSpec as P

MESH = pl.DeviceIdType.MESH
F32 = jnp.float32
BF16 = jnp.bfloat16

STAMP = 32
TAPS = 17
SIDE = 48
NB = 43
REACH = 4


def lanes(shape):
    return lax.broadcasted_iota(jnp.int32, shape, len(shape) - 1)


def inverse_4x4(m):
    p, q, s = m[0][0], m[0][1], m[1][1]
    i = 1.0 / (p * s - q * q)
    a, b, c = s * i, -q * i, p * i
    e, f, g, h = m[0][2], m[0][3], m[1][2], m[1][3]
    ae, af = a * e + b * g, a * f + b * h
    ce, cf = b * e + c * g, b * f + c * h
    t = m[2][2] - (e * ae + g * ce)
    u = m[2][3] - (e * af + g * cf)
    w = m[3][3] - (f * af + h * cf)
    j = 1.0 / (t * w - u * u)
    x, y, z = w * j, -u * j, t * j
    r00, r01 = -(ae * x + af * y), -(ae * y + af * z)
    r10, r11 = -(ce * x + cf * y), -(ce * y + cf * z)
    n00 = a - (r00 * ae + r01 * af)
    n01 = b - (r00 * ce + r01 * cf)
    n11 = c - (r10 * ce + r11 * cf)
    return (
        (n00, n01, r00, r01),
        (n01, n11, r10, r11),
        (r00, r10, x, y),
        (r01, r11, y, z),
    )


def solve(tiles):
    lane = lanes((8, 128))
    tiles = list(tiles)
    for block in range(11):
        first = 4 * block
        tile = tiles[first // 8]
        rows = [
            jnp.broadcast_to(tile[(first + c) % 8 : (first + c) % 8 + 1, :], (8, 128))
            for c in range(4)
        ]
        pivot = [[None] * 4 for _ in range(4)]
        for r in range(4):
            for c in range(r, 4):
                value = jnp.broadcast_to(rows[r][:, first + c : first + c + 1], (8, 128))
                pivot[r][c] = pivot[c][r] = value
        inverse = inverse_4x4(pivot)
        inside = (lane >= first) & (lane < first + 4)
        rows = [
            jnp.where(inside, jnp.where(lane == first + c, -1.0, 0.0), rows[c])
            for c in range(4)
        ]
        scaled = [
            (inverse[r][0] * rows[0] + inverse[r][1] * rows[1])
            + (inverse[r][2] * rows[2] + inverse[r][3] * rows[3])
            for r in range(4)
        ]
        for t in range((first + 4) // 8, 6):
            old = tiles[t]
            cols = [
                jnp.broadcast_to(old[:, first + c : first + c + 1], (8, 128))
                for c in range(4)
            ]
            change = (cols[0] * scaled[0] + cols[1] * scaled[1]) + (
                cols[2] * scaled[2] + cols[3] * scaled[3]
            )
            tiles[t] = jnp.where(inside, 0.0, old) - change
    return tiles[5][7:8, :]


def unpack(low, high, right):
    lane = lanes((8, 128))
    row = lax.broadcasted_iota(jnp.int32, (8, 128), 0)
    tiles = [low, high]
    tiles += [pltpu.roll(x, 96, 1) for x in (low, high)]
    tiles += [pltpu.roll(x, 80, 1) for x in (low, high)]
    full = jnp.concatenate(tiles, axis=0)
    keep = lanes((SIDE, 128)) // 16 >= lax.broadcasted_iota(jnp.int32, (SIDE, 128), 0) // 16
    upper = jnp.where(keep & (lanes((SIDE, 128)) < SIDE), full, 0.0)
    square = jnp.concatenate([upper, jnp.zeros((128 - SIDE, 128), F32)], axis=0)
    flipped = square.T[:SIDE]
    full = jnp.where(keep, upper, flipped)
    tiles = [full[8 * t : 8 * t + 8] for t in range(6)]
    right = jnp.broadcast_to(right, (8, 128))
    right = jnp.where(lane < NB, right, 0.0)
    tiles[5] = jnp.where(row == 7, right, tiles[5])
    tiles[5] = jnp.where((row == 3) & (lane == NB), 1.0, tiles[5])
    return tiles


def kernel(
    visits,
    patches,
    template_ref,
    across_ref,
    down_ref,
    weight_ref,
    patch_ref,
    science_ref,
    coef_ref,
    residual_ref,
    template_own,
    across_own,
    down_own,
    weight_own,
    patch_own,
    across_scr,
    down_scr,
    turn_scr,
    choice_scr,
    w_own,
    rows_scr,
    wide_scr,
    image_scr,
    sci_recv,
    sci_scr,
    w_recv,
    gram_scr,
    msg,
    inbox,
    side_msg,
    side_inbox,
    near_msg,
    near_inbox,
    coef_row,
    coef_box,
    own_sem,
    small_sem,
    sci_send,
    sci_sem,
    w_send,
    w_sem,
    msg_send,
    msg_sem,
    side_send,
    side_sem,
    near_send,
    near_sem,
    coef_send,
    coef_sem,
    row_send,
    row_sem,
):
    me_v = lax.axis_index("visit")
    me_q = lax.axis_index("patch")
    barrier = pltpu.get_barrier_semaphore()

    def visit_peer(step):
        return lax.rem(me_v + step, visits), me_q

    def patch_peer(step):
        return me_v, lax.rem(me_q + step + patches, patches)

    side_v = lax.rem(me_v, 2)
    chip = lax.div(me_v, 2)
    partner = (me_v + 1 - 2 * side_v, me_q)

    def rank(v):
        return 4 * lax.rem(v, 2) + lax.div(v, 2)

    others = range(1, 8)
    around = (-2, -1, 1, 2)

    small = [
        pltpu.make_async_copy(source, target, small_sem.at[n])
        for n, (source, target) in enumerate(
            (
                (weight_ref, weight_own),
                (across_ref, across_own),
                (down_ref, down_own),
                (patch_ref, patch_own),
                (template_ref, template_own),
            )
        )
    ]
    for copy in small:
        copy.start()

    for peer in [visit_peer(j) for j in others] + [patch_peer(j) for j in around]:
        pl.semaphore_signal(barrier, inc=1, device_id=peer, device_id_type=MESH)

    own_copy = pltpu.make_async_copy(science_ref.at[0, 0, me_v], sci_recv.at[rank(me_v)], own_sem)
    own_copy.start()
    for copy in small:
        copy.wait()
    w_own[...] = jnp.concatenate(
        [weight_own[0, 0].astype(F32), jnp.zeros((8, 112), F32)], axis=1
    )
    w_recv[pl.ds(rank(me_v), 1), :] = w_own[pl.ds(me_v, 1), :]
    tap = lax.broadcasted_iota(jnp.int32, (TAPS, 128), 0)
    column = lanes((TAPS, 128)) % STAMP
    backwards = ((column + tap) % STAMP == 0).astype(F32).astype(BF16)
    forwards = (column == tap).astype(F32).astype(BF16)
    nothing5 = jnp.zeros((5, 128), F32)
    across_scr[NB:, :] = nothing5
    first_axes = (((0,), (0,)), ((), ()))
    across_scr[0:NB, :] = lax.dot_general(
        across_own[...].astype(BF16), backwards, first_axes, preferred_element_type=F32
    )
    down_scr[NB:, :] = nothing5
    down_scr[0:NB, :] = lax.dot_general(
        down_own[...].astype(BF16), forwards, first_axes, preferred_element_type=F32
    )
    near = jnp.concatenate([patch_own[0], jnp.zeros((1, 112), jnp.int32)], axis=1)
    near = lax.rem(near - me_q + 1 + patches, patches).astype(F32)
    near16 = jnp.broadcast_to(near, (16, 128))
    diagonal = lanes((16, 128)) == lax.broadcasted_iota(jnp.int32, (16, 128), 0)
    choice_scr[...] = jnp.broadcast_to(
        jnp.sum(jnp.where(diagonal, near16, 0.0), axis=1, keepdims=True), (16, 128)
    )
    flat = template_own[0, 0].astype(F32)
    for z in range(SIDE):
        turn_scr[16 * z : 16 * z + 16, 0:SIDE] = flat[:, SIDE * z : SIDE * z + SIDE]
    stamps = jnp.concatenate(
        [
            jnp.concatenate(
                [
                    turn_scr[pl.ds(4 * g + s, SIDE, stride=16), :][:, :SIDE]
                    for s in range(4)
                ],
                axis=1,
            )
            for g in range(4)
        ],
        axis=0,
    ).astype(BF16)
    pl.semaphore_wait(barrier, len(others) + len(around))

    def send(source, target, sems, peer):
        pltpu.make_async_remote_copy(
            src_ref=source,
            dst_ref=target,
            send_sem=sems[0],
            recv_sem=sems[1],
            device_id=peer,
            device_id_type=MESH,
        ).start()

    def wait(like, sem):
        pltpu.make_async_copy(like, like, sem).wait()

    for j in (4, 3, 5, 2, 6, 1, 7):
        peer = visit_peer(j)
        send(
            science_ref.at[0, 0, peer[0]],
            sci_recv.at[rank(me_v)],
            (sci_send, sci_sem),
            peer,
        )
    for j in (4, 3, 5, 2, 6, 1, 7):
        peer = visit_peer(j)
        send(
            w_own.at[pl.ds(peer[0], 1), :],
            w_recv.at[pl.ds(rank(me_v), 1), :],
            (w_send, w_sem),
            peer,
        )

    shape = (SIDE, 128)
    past = lax.broadcasted_iota(jnp.int32, shape, 0) - lanes(shape) % STAMP
    band = (past >= 0) & (past < TAPS)
    masks = [
        (band & (lanes(shape) // STAMP == s)).astype(F32).astype(BF16) for s in range(4)
    ]
    rows_scr[44:48] = jnp.zeros((4, SIDE, 512), BF16)

    @pl.loop(0, 22, unroll=22)
    def make_rows(pair):
        right = []
        for j in range(2):
            taps = across_scr[pl.ds(2 * pair + j, 1), :]
            table = pltpu.roll(
                jnp.broadcast_to(taps, (STAMP, 128)), 0, 1, stride=1, stride_axis=0
            )
            table = jnp.concatenate([table, table[: SIDE - STAMP]], axis=0).astype(BF16)
            right.append(jnp.concatenate([table * m for m in masks], axis=0))
        right = jnp.concatenate(right, axis=1)
        out = jnp.dot(stamps, right, preferred_element_type=F32).astype(BF16)
        for j in range(2):
            for g in range(4):
                rows_scr[2 * pair + j, :, 128 * g : 128 * g + 128] = out[
                    SIDE * g : SIDE * g + SIDE, 128 * j : 128 * j + 128
                ]

    within = lanes((8, 128)) // STAMP - lax.broadcasted_iota(jnp.int32, (8, 128), 0)
    owner, owner4 = within == 0, within == -4

    @pl.loop(0, 6, unroll=6)
    def make_images(group):
        first = pl.multiple_of(group * 8, 8)
        taps = down_scr[pl.ds(first, 8), :]
        left = jnp.concatenate(
            [jnp.where(owner, taps, 0.0), jnp.where(owner4, taps, 0.0)], axis=1
        )
        left = jnp.concatenate(
            [left]
            + [
                jnp.concatenate(
                    [
                        pltpu.roll(left[:, :128], y, 1),
                        pltpu.roll(left[:, 128:], y, 1),
                    ],
                    axis=1,
                )
                for y in range(1, 16)
            ],
            axis=0,
        ).astype(BF16)
        for half in range(2):
            right = rows_scr[pl.ds(first, 8), 16 * half : 16 * half + 32, :]
            out = jnp.dot(left, right.reshape(256, 512), preferred_element_type=F32)
            wide_scr[16 * half : 16 * half + 16, pl.ds(first, 8), :] = out.reshape(16, 8, 512)

    lane = lanes((SIDE, 128))
    even = lane // STAMP % 2 == 0
    lower = lane < 64

    @pl.loop(0, 8, unroll=8)
    def regroup(quad):
        for g in range(4):
            part = [
                wide_scr[4 * quad + r, :, 128 * g : 128 * g + 128] for r in range(4)
            ]
            for a, b in ((0, 1), (2, 3)):
                x, y = part[a], part[b]
                part[a] = jnp.where(even, x, pltpu.roll(y, 32, 1))
                part[b] = jnp.where(even, pltpu.roll(x, 96, 1), y)
            for a, b in ((0, 2), (1, 3)):
                x, y = part[a], part[b]
                part[a] = jnp.where(lower, x, pltpu.roll(y, 64, 1))
                part[b] = jnp.where(lower, pltpu.roll(x, 64, 1), y)
            for s in range(4):
                image_scr[4 * g + s, :, pl.ds(pl.multiple_of(quad * 128, 128), 128)] = part[
                    s
                ].astype(BF16)

    lane16 = lanes((16, 128))
    second_axes = (((1,), (1,)), ((), ()))

    @pl.loop(0, 16, unroll=16)
    def make_grams(s):
        image = image_scr[s]
        out = lax.dot_general(image, image, second_axes, preferred_element_type=F32)
        out = jnp.concatenate([out, jnp.zeros((SIDE, 80), F32)], axis=1)
        packed = jnp.where(
            lane16 < 48,
            out[0:16],
            jnp.where(
                lane16 < 80,
                pltpu.roll(out[16:32], 32, 1),
                pltpu.roll(out[32:48], 48, 1),
            ),
        )
        gram_scr[pl.ds(pl.multiple_of(s * 16, 16), 16), :] = packed

    wait(w_recv.at[1:], w_sem)
    weights = w_recv[...]
    offset = near16[0:8]
    weighted = [jnp.where(offset == float(o), weights, 0.0) for o in range(REACH)]
    left = jnp.concatenate(weighted, axis=0)[:, :16].astype(BF16)
    left = jnp.concatenate([left] * 3, axis=1)
    right = jnp.concatenate(
        [gram_scr[pl.ds(r, 16, stride=16), :] for r in range(16)], axis=1
    )
    top = right.astype(BF16)
    rest = right - top.astype(F32)
    middle = rest.astype(BF16)
    low = (rest - middle.astype(F32)).astype(BF16)
    systems = jnp.dot(
        left, jnp.concatenate([top, middle, low], axis=0), preferred_element_type=F32
    )
    for r in range(16):
        for o in range(REACH):
            msg[pl.ds(16 * o + r, 8, stride=64), :] = systems[
                8 * o : 8 * o + 8, 128 * r : 128 * r + 128
            ]

    def part(n, size):
        return pl.ds(pl.multiple_of(n * size, size), size)

    send(msg.at[part(1 - side_v, 256), :], inbox, (msg_send, msg_sem), partner)

    own_copy.wait()
    wait(sci_recv.at[1:], sci_sem)
    for v in range(8):
        for t in range(8):
            sci_scr[128 * t + 16 * v : 128 * t + 16 * v + 16, :] = sci_recv[
                v, :, 128 * t : 128 * t + 128
            ].astype(F32)

    def exposures(s):
        return [sci_scr[pl.ds(128 * t + s, 8, stride=16), :] for t in range(8)]

    sides = [jnp.zeros((8, SIDE), F32) for _ in range(REACH)]
    for s in range(16):
        science = jnp.concatenate(exposures(s), axis=1).astype(BF16)
        out = lax.dot_general(
            science, image_scr[s], second_axes, preferred_element_type=F32
        )
        for o in range(REACH):
            factor = jnp.broadcast_to(weighted[o][:, s : s + 1], (8, SIDE))
            sides[o] = sides[o] + factor * out
    for o in range(REACH):
        side_msg[pl.ds(o, 8, stride=8), :] = jnp.concatenate(
            [sides[o], jnp.zeros((8, 80), F32)], axis=1
        )
        side_msg[pl.ds(4 + o, 8, stride=8), :] = jnp.zeros((8, 128), F32)
    send(
        side_msg.at[part(1 - side_v, 32), :], side_inbox, (side_send, side_sem), partner
    )

    wait(inbox, msg_sem)
    summed = msg[part(side_v, 256), :] + inbox[...]
    for n in range(16):
        near_msg[n, 0:16, :] = summed[16 * n : 16 * n + 16]
    wait(side_inbox, side_sem)
    summed = side_msg[part(side_v, 32), :] + side_inbox[...]
    for n in range(16):
        row = 8 * (n // 4) + n % 4
        near_msg[n, 16:17, :] = summed[row : row + 1]
    near = [(o, j) for o in range(REACH) for j in range(4) if (o, j) != (1, 0)]
    near.sort(key=lambda t: -abs(t[0] - 1) - min(t[1], 4 - t[1]))
    for o, j in near:
        there = lax.rem(chip + j, 4)
        send(
            near_msg.at[4 * there + o],
            near_inbox.at[4 * o + j],
            (near_send, near_sem),
            (2 * there + side_v, patch_peer(o - 1)[1]),
        )
    total = near_msg[4 * chip + 1]
    wait(near_inbox.at[1:], near_sem)
    for o, j in near:
        total = total + near_inbox[4 * o + j]

    answer = solve(unpack(total[0:8], total[8:16], total[16:17]))
    answer = jnp.where(lanes((1, 128)) < NB, answer, 0.0)
    coef_row[pl.ds(side_v, 1), :] = answer
    mine = pl.ds(side_v, 1)
    send(coef_row.at[mine, :], coef_row.at[mine, :], (coef_send, coef_sem), partner)
    coef_ref[0] = answer[:, :NB]
    wait(coef_row.at[0:1], coef_sem)
    for o, j in near:
        there = lax.rem(chip + j, 4)
        send(
            coef_row,
            coef_box.at[o, chip],
            (row_send, row_sem),
            (2 * there + side_v, patch_peer(1 - o)[1]),
        )
    coef_box[1, chip] = coef_row[...]
    wait(inbox.at[0:30], row_sem)
    coefs_of = [
        jnp.concatenate(
            [coef_box[o, x, c : c + 1, :] for c in range(2) for x in range(4)], axis=0
        )
        for o in range(REACH)
    ]

    lane8 = lanes((8, 128))

    def fit(s, held):
        choice = jnp.broadcast_to(choice_scr[pl.ds(s, 1), :], (8, 128))
        coefs = coefs_of[0]
        for o in range(1, REACH):
            coefs = jnp.where(choice == float(o), coefs_of[o], coefs)
        model = jnp.dot(
            coefs[:, :SIDE].astype(BF16), image_scr[s], preferred_element_type=F32
        )
        diff = jnp.concatenate(exposures(s), axis=1) - model
        square = diff * diff
        part = square[:, 0:128]
        for t in range(1, 8):
            part = part + square[:, 128 * t : 128 * t + 128]
        return jnp.where(lane8 == s, jnp.sum(part, axis=1, keepdims=True), held)

    held = lax.fori_loop(0, 16, fit, jnp.zeros((8, 128), F32), unroll=16)
    held = held * weights * (1.0 / 1024.0)
    for v in range(8):
        row = 4 * (v % 2) + v // 2
        residual_ref[v, 0] = held[row : row + 1, :16]

    wait(w_recv.at[1:], w_send)
    wait(sci_recv.at[1:], sci_send)
    wait(inbox, msg_send)
    wait(side_inbox, side_send)
    wait(near_inbox.at[1:], near_send)
    wait(coef_row.at[0:1], coef_send)
    wait(inbox.at[0:30], row_send)


def on_device(template, science, weight, stamp_patch, basis_across, basis_down):
    visits = lax.axis_size("visit")
    patches = lax.axis_size("patch")
    vmem = pl.BlockSpec(memory_space=pltpu.VMEM)
    dma = pltpu.SemaphoreType.DMA
    return pl.pallas_call(
        functools.partial(kernel, visits, patches),
        out_shape=(
            jax.ShapeDtypeStruct((1, 1, NB), F32),
            jax.ShapeDtypeStruct((8, 1, 1, 16), F32),
        ),
        in_specs=[pl.BlockSpec(memory_space=pltpu.HBM)] * 6,
        out_specs=(vmem, vmem),
        scratch_shapes=[
            pltpu.VMEM(template.shape, BF16),
            pltpu.VMEM((TAPS, NB), F32),
            pltpu.VMEM((TAPS, NB), F32),
            pltpu.VMEM(weight.shape, BF16),
            pltpu.VMEM(stamp_patch.shape, jnp.int32),
            pltpu.VMEM((SIDE, 128), F32),
            pltpu.VMEM((SIDE, 128), F32),
            pltpu.VMEM((SIDE * 16, 128), F32),
            pltpu.VMEM((16, 128), F32),
            pltpu.VMEM((8, 128), F32),
            pltpu.VMEM((48, SIDE, 512), BF16),
            pltpu.VMEM((STAMP, SIDE, 512), F32),
            pltpu.VMEM((16, SIDE, 1024), BF16),
            pltpu.VMEM((8, 16, 1024), BF16),
            pltpu.VMEM((1024, 128), F32),
            pltpu.VMEM((8, 128), F32),
            pltpu.VMEM((256, 128), F32),
            pltpu.VMEM((512, 128), F32),
            pltpu.VMEM((256, 128), F32),
            pltpu.VMEM((64, 128), F32),
            pltpu.VMEM((32, 128), F32),
            pltpu.VMEM((16, 17, 128), F32),
            pltpu.VMEM((16, 17, 128), F32),
            pltpu.VMEM((2, 128), F32),
            pltpu.VMEM((REACH, 4, 2, 128), F32),
        ]
        + [dma, dma((5,))] + [dma] * 14,
        compiler_params=pltpu.CompilerParams(
            collective_id=0, has_side_effects=True, vmem_limit_bytes=60 * 1024 * 1024
        ),
    )(template, basis_across.T, basis_down.T, weight, stamp_patch, science)


def solution(mesh):
    return jax.shard_map(
        on_device,
        mesh=mesh,
        in_specs=(
            P("patch", "visit", None, None),
            P("visit", "patch", None, None, None),
            P("visit", "patch", None, None),
            P("patch", "visit", None),
            P(),
            P(),
        ),
        out_specs=(P("visit", "patch", None), P(None, "patch", "visit", None)),
        check_vma=False,
    )
```

```python
import functools

import jax
import jax.numpy as jnp
from jax import lax
from jax.experimental import pallas as pl
from jax.experimental.pallas import tpu as pltpu
from jax.sharding import PartitionSpec as P

MESH = pl.DeviceIdType.MESH
F32 = jnp.float32
BF16 = jnp.bfloat16

STAMP = 32
TAPS = 17
SIDE = 48
NB = 43
REACH = 4


def lanes(shape):
    return lax.broadcasted_iota(jnp.int32, shape, len(shape) - 1)


def inverse_4x4(m):
    p, q, s = m[0][0], m[0][1], m[1][1]
    i = 1.0 / (p * s - q * q)
    a, b, c = s * i, -q * i, p * i
    e, f, g, h = m[0][2], m[0][3], m[1][2], m[1][3]
    ae, af = a * e + b * g, a * f + b * h
    ce, cf = b * e + c * g, b * f + c * h
    t = m[2][2] - (e * ae + g * ce)
    u = m[2][3] - (e * af + g * cf)
    w = m[3][3] - (f * af + h * cf)
    j = 1.0 / (t * w - u * u)
    x, y, z = w * j, -u * j, t * j
    r00, r01 = -(ae * x + af * y), -(ae * y + af * z)
    r10, r11 = -(ce * x + cf * y), -(ce * y + cf * z)
    n00 = a - (r00 * ae + r01 * af)
    n01 = b - (r00 * ce + r01 * cf)
    n11 = c - (r10 * ce + r11 * cf)
    return (
        (n00, n01, r00, r01),
        (n01, n11, r10, r11),
        (r00, r10, x, y),
        (r01, r11, y, z),
    )


def invert(tiles):
    lane = lanes((8, 128))
    row = lax.broadcasted_iota(jnp.int32, (8, 128), 0)
    tiles = list(tiles)
    for block in range(11):
        first = 4 * block
        home, place = first // 8, first % 8
        rows = [
            jnp.broadcast_to(tiles[home][place + c : place + c + 1, :], (8, 128))
            for c in range(4)
        ]
        pivot = [[None] * 4 for _ in range(4)]
        for r in range(4):
            for c in range(r, 4):
                value = jnp.broadcast_to(rows[r][:, first + c : first + c + 1], (8, 128))
                pivot[r][c] = pivot[c][r] = value
        inverse = inverse_4x4(pivot)
        inside = (lane >= first) & (lane < first + 4)
        rows = [
            jnp.where(inside, jnp.where(lane == first + c, -1.0, 0.0), rows[c])
            for c in range(4)
        ]
        scaled = [
            (inverse[r][0] * rows[0] + inverse[r][1] * rows[1])
            + (inverse[r][2] * rows[2] + inverse[r][3] * rows[3])
            for r in range(4)
        ]
        for t in range(6):
            old = tiles[t]
            cols = [
                jnp.broadcast_to(old[:, first + c : first + c + 1], (8, 128))
                for c in range(4)
            ]
            change = (cols[0] * scaled[0] + cols[1] * scaled[1]) + (
                cols[2] * scaled[2] + cols[3] * scaled[3]
            )
            new = jnp.where(inside, 0.0, old) - change
            if t == home:
                for r in range(4):
                    new = jnp.where(row == place + r, -scaled[r], new)
            tiles[t] = new
    return tiles


def unpack(low, high):
    lane = lanes((8, 128))
    row = lax.broadcasted_iota(jnp.int32, (8, 128), 0)
    tiles = [low, high]
    tiles += [pltpu.roll(x, 96, 1) for x in (low, high)]
    tiles += [pltpu.roll(x, 80, 1) for x in (low, high)]
    full = jnp.concatenate(tiles, axis=0)
    keep = lanes((SIDE, 128)) // 16 >= lax.broadcasted_iota(jnp.int32, (SIDE, 128), 0) // 16
    upper = jnp.where(keep & (lanes((SIDE, 128)) < SIDE), full, 0.0)
    square = jnp.concatenate([upper, jnp.zeros((128 - SIDE, 128), F32)], axis=0)
    flipped = square.T[:SIDE]
    full = jnp.where(keep, upper, flipped)
    tiles = [full[8 * t : 8 * t + 8] for t in range(6)]
    tiles[5] = jnp.where((row == 3) & (lane == NB), 1.0, tiles[5])
    return tiles


def kernel(
    visits,
    patches,
    template_ref,
    across_ref,
    down_ref,
    weight_ref,
    patch_ref,
    science_ref,
    coef_ref,
    residual_ref,
    template_own,
    across_own,
    down_own,
    weight_own,
    patch_own,
    across_scr,
    down_scr,
    turn_scr,
    choice_scr,
    w_own,
    rows_scr,
    wide_scr,
    image_scr,
    sci_recv,
    sci_scr,
    w_recv,
    gram_scr,
    msg,
    inbox,
    side_msg,
    side_near,
    near_msg,
    near_inbox,
    coef_row,
    coef_box,
    own_sem,
    small_sem,
    sci_send,
    sci_sem,
    w_send,
    w_sem,
    msg_send,
    msg_sem,
    near_send,
    near_sem,
    near_side_send,
    near_side_sem,
    row_send,
    row_sem,
):
    me_v = lax.axis_index("visit")
    me_q = lax.axis_index("patch")
    barrier = pltpu.get_barrier_semaphore()

    def visit_peer(step):
        return lax.rem(me_v + step, visits), me_q

    def patch_peer(step):
        return me_v, lax.rem(me_q + step + patches, patches)

    side_v = lax.rem(me_v, 2)
    chip = lax.div(me_v, 2)
    partner = (me_v + 1 - 2 * side_v, me_q)

    def rank(v):
        return 4 * lax.rem(v, 2) + lax.div(v, 2)

    others = range(1, 8)
    around = (-2, -1, 1, 2)

    order = (4, 3, 5, 2, 6, 1, 7)
    for peer in [visit_peer(j) for j in order] + [patch_peer(j) for j in around]:
        pl.semaphore_signal(barrier, inc=1, device_id=peer, device_id_type=MESH)

    small = [
        pltpu.make_async_copy(source, target, small_sem.at[n])
        for n, (source, target) in enumerate(
            (
                (weight_ref, weight_own),
                (across_ref, across_own),
                (down_ref, down_own),
                (patch_ref, patch_own),
                (template_ref, template_own),
            )
        )
    ]
    for copy in small:
        copy.start()

    own_copy = pltpu.make_async_copy(science_ref.at[0, 0, me_v], sci_recv.at[rank(me_v)], own_sem)
    own_copy.start()
    for copy in small:
        copy.wait()
    w_own[...] = jnp.concatenate(
        [weight_own[0, 0].astype(F32), jnp.zeros((8, 112), F32)], axis=1
    )
    w_recv[pl.ds(rank(me_v), 1), :] = w_own[pl.ds(me_v, 1), :]
    tap = lax.broadcasted_iota(jnp.int32, (TAPS, 128), 0)
    column = lanes((TAPS, 128)) % STAMP
    backwards = ((column + tap) % STAMP == 0).astype(F32).astype(BF16)
    forwards = (column == tap).astype(F32).astype(BF16)
    nothing5 = jnp.zeros((5, 128), F32)
    across_scr[NB:, :] = nothing5
    first_axes = (((0,), (0,)), ((), ()))
    across_scr[0:NB, :] = lax.dot_general(
        across_own[...].astype(BF16), backwards, first_axes, preferred_element_type=F32
    )
    down_scr[NB:, :] = nothing5
    down_scr[0:NB, :] = lax.dot_general(
        down_own[...].astype(BF16), forwards, first_axes, preferred_element_type=F32
    )
    near = jnp.concatenate([patch_own[0], jnp.zeros((1, 112), jnp.int32)], axis=1)
    near = lax.rem(near - me_q + 1 + patches, patches).astype(F32)
    near16 = jnp.broadcast_to(near, (16, 128))
    diagonal = lanes((16, 128)) == lax.broadcasted_iota(jnp.int32, (16, 128), 0)
    choice_scr[...] = jnp.broadcast_to(
        jnp.sum(jnp.where(diagonal, near16, 0.0), axis=1, keepdims=True), (16, 128)
    )
    flat = template_own[0, 0].astype(F32)
    for z in range(SIDE):
        turn_scr[16 * z : 16 * z + 16, 0:SIDE] = flat[:, SIDE * z : SIDE * z + SIDE]
    stamps = jnp.concatenate(
        [
            jnp.concatenate(
                [
                    turn_scr[pl.ds(4 * g + s, SIDE, stride=16), :][:, :SIDE]
                    for s in range(4)
                ],
                axis=1,
            )
            for g in range(4)
        ],
        axis=0,
    ).astype(BF16)
    pl.semaphore_wait(barrier, len(others) + len(around))

    def send(source, target, sems, peer):
        pltpu.make_async_remote_copy(
            src_ref=source,
            dst_ref=target,
            send_sem=sems[0],
            recv_sem=sems[1],
            device_id=peer,
            device_id_type=MESH,
        ).start()

    def wait(like, sem):
        pltpu.make_async_copy(like, like, sem).wait()

    for j in order:
        peer = visit_peer(j)
        send(
            w_own.at[pl.ds(peer[0], 1), :],
            w_recv.at[pl.ds(rank(me_v), 1), :],
            (w_send, w_sem),
            peer,
        )
    for j in order:
        peer = visit_peer(j)
        send(
            science_ref.at[0, 0, peer[0]],
            sci_recv.at[rank(me_v)],
            (sci_send, sci_sem),
            peer,
        )

    shape = (SIDE, 128)
    past = lax.broadcasted_iota(jnp.int32, shape, 0) - lanes(shape) % STAMP
    band = (past >= 0) & (past < TAPS)
    masks = [
        (band & (lanes(shape) // STAMP == s)).astype(F32).astype(BF16) for s in range(4)
    ]
    rows_scr[44:48] = jnp.zeros((4, SIDE, 512), BF16)

    @pl.loop(0, 22, unroll=22)
    def make_rows(pair):
        right = []
        for j in range(2):
            taps = across_scr[pl.ds(2 * pair + j, 1), :]
            table = pltpu.roll(
                jnp.broadcast_to(taps, (STAMP, 128)), 0, 1, stride=1, stride_axis=0
            )
            table = jnp.concatenate([table, table[: SIDE - STAMP]], axis=0).astype(BF16)
            right.append(jnp.concatenate([table * m for m in masks], axis=0))
        right = jnp.concatenate(right, axis=1)
        out = jnp.dot(stamps, right, preferred_element_type=F32).astype(BF16)
        for j in range(2):
            for g in range(4):
                rows_scr[2 * pair + j, :, 128 * g : 128 * g + 128] = out[
                    SIDE * g : SIDE * g + SIDE, 128 * j : 128 * j + 128
                ]

    within = lanes((8, 128)) // STAMP - lax.broadcasted_iota(jnp.int32, (8, 128), 0)
    owner, owner4 = within == 0, within == -4

    @pl.loop(0, 6, unroll=6)
    def make_images(group):
        first = pl.multiple_of(group * 8, 8)
        taps = down_scr[pl.ds(first, 8), :]
        left = jnp.concatenate(
            [jnp.where(owner, taps, 0.0), jnp.where(owner4, taps, 0.0)], axis=1
        )
        left = jnp.concatenate(
            [left]
            + [
                jnp.concatenate(
                    [
                        pltpu.roll(left[:, :128], y, 1),
                        pltpu.roll(left[:, 128:], y, 1),
                    ],
                    axis=1,
                )
                for y in range(1, 16)
            ],
            axis=0,
        ).astype(BF16)
        for half in range(2):
            right = rows_scr[pl.ds(first, 8), 16 * half : 16 * half + 32, :]
            out = jnp.dot(left, right.reshape(256, 512), preferred_element_type=F32)
            wide_scr[16 * half : 16 * half + 16, pl.ds(first, 8), :] = out.reshape(16, 8, 512)

    lane = lanes((SIDE, 128))
    even = lane // STAMP % 2 == 0
    lower = lane < 64

    @pl.loop(0, 8, unroll=8)
    def regroup(quad):
        for g in range(4):
            part = [
                wide_scr[4 * quad + r, :, 128 * g : 128 * g + 128] for r in range(4)
            ]
            for a, b in ((0, 1), (2, 3)):
                x, y = part[a], part[b]
                part[a] = jnp.where(even, x, pltpu.roll(y, 32, 1))
                part[b] = jnp.where(even, pltpu.roll(x, 96, 1), y)
            for a, b in ((0, 2), (1, 3)):
                x, y = part[a], part[b]
                part[a] = jnp.where(lower, x, pltpu.roll(y, 64, 1))
                part[b] = jnp.where(lower, pltpu.roll(x, 64, 1), y)
            for s in range(4):
                image_scr[4 * g + s, :, pl.ds(pl.multiple_of(quad * 128, 128), 128)] = part[
                    s
                ].astype(BF16)

    lane16 = lanes((16, 128))
    second_axes = (((1,), (1,)), ((), ()))

    @pl.loop(0, 16, unroll=16)
    def make_grams(s):
        image = image_scr[s]
        out = lax.dot_general(image, image, second_axes, preferred_element_type=F32)
        out = jnp.concatenate([out, jnp.zeros((SIDE, 80), F32)], axis=1)
        packed = jnp.where(
            lane16 < 48,
            out[0:16],
            jnp.where(
                lane16 < 80,
                pltpu.roll(out[16:32], 32, 1),
                pltpu.roll(out[32:48], 48, 1),
            ),
        )
        gram_scr[pl.ds(pl.multiple_of(s * 16, 16), 16), :] = packed

    wait(w_recv.at[1:], w_sem)
    weights = w_recv[...]
    offset = near16[0:8]
    weighted = [jnp.where(offset == float(o), weights, 0.0) for o in range(REACH)]
    left = jnp.concatenate(weighted, axis=0)[:, :16].astype(BF16)
    left = jnp.concatenate([left] * 3, axis=1)
    right = jnp.concatenate(
        [gram_scr[pl.ds(r, 16, stride=16), :] for r in range(16)], axis=1
    )
    top = right.astype(BF16)
    rest = right - top.astype(F32)
    middle = rest.astype(BF16)
    low = (rest - middle.astype(F32)).astype(BF16)
    systems = jnp.dot(
        left, jnp.concatenate([top, middle, low], axis=0), preferred_element_type=F32
    )
    for r in range(16):
        for o in range(REACH):
            msg[pl.ds(16 * o + r, 8, stride=64), :] = systems[
                8 * o : 8 * o + 8, 128 * r : 128 * r + 128
            ]

    def part(n, size):
        return pl.ds(pl.multiple_of(n * size, size), size)

    send(msg.at[part(1 - side_v, 256), :], inbox, (msg_send, msg_sem), partner)

    near = [(o, j) for o in range(REACH) for j in range(4) if (o, j) != (1, 0)]
    near.sort(key=lambda t: -abs(t[0] - 1) - min(t[1], 4 - t[1]))
    wait(inbox, msg_sem)
    summed = msg[part(side_v, 256), :] + inbox[...]
    for n in range(16):
        near_msg[n] = summed[16 * n : 16 * n + 16]
    for o, j in near:
        there = lax.rem(chip + j, 4)
        send(
            near_msg.at[4 * there + o],
            near_inbox.at[4 * o + j],
            (near_send, near_sem),
            (2 * there + side_v, patch_peer(o - 1)[1]),
        )

    own_copy.wait()
    wait(sci_recv.at[1:], sci_sem)
    for v in range(8):
        for t in range(8):
            sci_scr[128 * t + 16 * v : 128 * t + 16 * v + 16, :] = sci_recv[
                v, :, 128 * t : 128 * t + 128
            ].astype(F32)

    def exposures(s):
        return [sci_scr[pl.ds(128 * t + s, 8, stride=16), :] for t in range(8)]

    sides = [jnp.zeros((8, SIDE), F32) for _ in range(REACH)]
    for s in range(16):
        science = jnp.concatenate(exposures(s), axis=1).astype(BF16)
        out = lax.dot_general(
            science, image_scr[s], second_axes, preferred_element_type=F32
        )
        for o in range(REACH):
            factor = jnp.broadcast_to(weighted[o][:, s : s + 1], (8, SIDE))
            sides[o] = sides[o] + factor * out
    for o in range(REACH):
        side_msg[pl.ds(o, 8, stride=8), :] = jnp.concatenate(
            [sides[o], jnp.zeros((8, 80), F32)], axis=1
        )
        side_msg[pl.ds(4 + o, 8, stride=8), :] = jnp.zeros((8, 128), F32)
    every = [(o, j) for o in range(REACH) for j in range(8) if (o, j) != (1, 0)]
    every.sort(key=lambda t: -abs(t[0] - 1) - (min(t[1], 8 - t[1]) + 1) // 2)
    for o, j in every:
        v = visit_peer(j)[0]
        send(
            side_msg.at[pl.ds(8 * rank(v) + o, 1), :],
            side_near.at[pl.ds(8 * o + j, 1), :],
            (near_side_send, near_side_sem),
            (v, patch_peer(o - 1)[1]),
        )

    total = near_msg[4 * chip + 1]
    wait(near_inbox.at[1:], near_sem)
    for o, j in near:
        total = total + near_inbox[4 * o + j]
    inverse = invert(unpack(total[0:8], total[8:16]))
    side_near[8:9, :] = side_msg[pl.ds(8 * rank(me_v) + 1, 1), :]
    wait(msg.at[0:31, :], near_side_sem)
    side = jnp.sum(side_near[...], axis=0, keepdims=True)
    side = jnp.where(lanes((1, 128)) < NB, side, 0.0)
    side = jnp.broadcast_to(side, (8, 128))
    across = lanes((8, 128)) - lax.broadcasted_iota(jnp.int32, (8, 128), 0)
    answer = jnp.zeros((8, 128), F32)
    for t in range(6):
        value = jnp.sum(inverse[t] * side, axis=1, keepdims=True)
        answer = answer + jnp.where(across == 8 * t, value, 0.0)
    answer = jnp.sum(answer, axis=0, keepdims=True)
    answer = jnp.where(lanes((1, 128)) < NB, answer, 0.0)
    coef_row[...] = answer
    place = pl.ds(rank(me_v), 1)
    for o, j in every:
        send(
            coef_row,
            coef_box.at[o, place, :],
            (row_send, row_sem),
            (visit_peer(j)[0], patch_peer(1 - o)[1]),
        )
    coef_ref[0] = answer[:, :NB]
    coef_box[1, place, :] = answer
    wait(msg.at[0:31, :], row_sem)

    lane8 = lanes((8, 128))

    def fit(s, held):
        choice = jnp.broadcast_to(choice_scr[pl.ds(s, 1), :], (8, 128))
        coefs = coef_box[0]
        for o in range(1, REACH):
            coefs = jnp.where(choice == float(o), coef_box[o], coefs)
        model = jnp.dot(
            coefs[:, :SIDE].astype(BF16), image_scr[s], preferred_element_type=F32
        )
        diff = jnp.concatenate(exposures(s), axis=1) - model
        square = diff * diff
        part = square[:, 0:128]
        for t in range(1, 8):
            part = part + square[:, 128 * t : 128 * t + 128]
        return jnp.where(lane8 == s, jnp.sum(part, axis=1, keepdims=True), held)

    held = lax.fori_loop(0, 16, fit, jnp.zeros((8, 128), F32), unroll=16)
    held = held * weights * (1.0 / 1024.0)
    for v in range(8):
        row = 4 * (v % 2) + v // 2
        residual_ref[v, 0] = held[row : row + 1, :16]

    wait(w_recv.at[1:], w_send)
    wait(sci_recv.at[1:], sci_send)
    wait(inbox, msg_send)
    wait(near_inbox.at[1:], near_send)
    wait(msg.at[0:31, :], near_side_send)
    wait(msg.at[0:31, :], row_send)


def on_device(template, science, weight, stamp_patch, basis_across, basis_down):
    visits = lax.axis_size("visit")
    patches = lax.axis_size("patch")
    vmem = pl.BlockSpec(memory_space=pltpu.VMEM)
    dma = pltpu.SemaphoreType.DMA
    return pl.pallas_call(
        functools.partial(kernel, visits, patches),
        out_shape=(
            jax.ShapeDtypeStruct((1, 1, NB), F32),
            jax.ShapeDtypeStruct((8, 1, 1, 16), F32),
        ),
        in_specs=[pl.BlockSpec(memory_space=pltpu.HBM)] * 6,
        out_specs=(vmem, vmem),
        scratch_shapes=[
            pltpu.VMEM(template.shape, BF16),
            pltpu.VMEM((TAPS, NB), F32),
            pltpu.VMEM((TAPS, NB), F32),
            pltpu.VMEM(weight.shape, BF16),
            pltpu.VMEM(stamp_patch.shape, jnp.int32),
            pltpu.VMEM((SIDE, 128), F32),
            pltpu.VMEM((SIDE, 128), F32),
            pltpu.VMEM((SIDE * 16, 128), F32),
            pltpu.VMEM((16, 128), F32),
            pltpu.VMEM((8, 128), F32),
            pltpu.VMEM((48, SIDE, 512), BF16),
            pltpu.VMEM((STAMP, SIDE, 512), F32),
            pltpu.VMEM((16, SIDE, 1024), BF16),
            pltpu.VMEM((8, 16, 1024), BF16),
            pltpu.VMEM((1024, 128), F32),
            pltpu.VMEM((8, 128), F32),
            pltpu.VMEM((256, 128), F32),
            pltpu.VMEM((512, 128), F32),
            pltpu.VMEM((256, 128), F32),
            pltpu.VMEM((64, 128), F32),
            pltpu.VMEM((32, 128), F32),
            pltpu.VMEM((16, 16, 128), F32),
            pltpu.VMEM((16, 16, 128), F32),
            pltpu.VMEM((1, 128), F32),
            pltpu.VMEM((REACH, 8, 128), F32),
        ]
        + [dma, dma((5,))] + [dma] * 12,
        compiler_params=pltpu.CompilerParams(
            collective_id=0, has_side_effects=True, vmem_limit_bytes=32 * 1024 * 1024
        ),
    )(
        *(
            pltpu.with_memory_space_constraint(x, pltpu.HBM)
            for x in (template, basis_across.T, basis_down.T, weight, stamp_patch, science)
        )
    )


def solution(mesh):
    return jax.shard_map(
        on_device,
        mesh=mesh,
        in_specs=(
            P("patch", "visit", None, None),
            P("visit", "patch", None, None, None),
            P("visit", "patch", None, None),
            P("patch", "visit", None),
            P(),
            P(),
        ),
        out_specs=(P("visit", "patch", None), P(None, "patch", "visit", None)),
        check_vma=False,
    )
```

```python
import functools

import jax
import jax.numpy as jnp
from jax import lax
from jax.experimental import pallas as pl
from jax.experimental.pallas import tpu as pltpu
from jax.sharding import PartitionSpec as P

MESH = pl.DeviceIdType.MESH
F32 = jnp.float32
BF16 = jnp.bfloat16

STAMP = 32
TAPS = 17
SIDE = 48
NB = 43
REACH = 4


def lanes(shape):
    return lax.broadcasted_iota(jnp.int32, shape, len(shape) - 1)


def inverse_4x4(m):
    p, q, s = m[0][0], m[0][1], m[1][1]
    i = 1.0 / (p * s - q * q)
    a, b, c = s * i, -q * i, p * i
    e, f, g, h = m[0][2], m[0][3], m[1][2], m[1][3]
    ae, af = a * e + b * g, a * f + b * h
    ce, cf = b * e + c * g, b * f + c * h
    t = m[2][2] - (e * ae + g * ce)
    u = m[2][3] - (e * af + g * cf)
    w = m[3][3] - (f * af + h * cf)
    j = 1.0 / (t * w - u * u)
    x, y, z = w * j, -u * j, t * j
    r00, r01 = -(ae * x + af * y), -(ae * y + af * z)
    r10, r11 = -(ce * x + cf * y), -(ce * y + cf * z)
    n00 = a - (r00 * ae + r01 * af)
    n01 = b - (r00 * ce + r01 * cf)
    n11 = c - (r10 * ce + r11 * cf)
    return (
        (n00, n01, r00, r01),
        (n01, n11, r10, r11),
        (r00, r10, x, y),
        (r01, r11, y, z),
    )


def invert(tiles):
    lane = lanes((8, 128))
    row = lax.broadcasted_iota(jnp.int32, (8, 128), 0)
    tiles = list(tiles)
    for block in range(11):
        first = 4 * block
        home, place = first // 8, first % 8
        rows = [
            jnp.broadcast_to(tiles[home][place + c : place + c + 1, :], (8, 128))
            for c in range(4)
        ]
        pivot = [[None] * 4 for _ in range(4)]
        for r in range(4):
            for c in range(r, 4):
                value = jnp.broadcast_to(rows[r][:, first + c : first + c + 1], (8, 128))
                pivot[r][c] = pivot[c][r] = value
        inverse = inverse_4x4(pivot)
        inside = (lane >= first) & (lane < first + 4)
        rows = [
            jnp.where(inside, jnp.where(lane == first + c, -1.0, 0.0), rows[c])
            for c in range(4)
        ]
        scaled = [
            (inverse[r][0] * rows[0] + inverse[r][1] * rows[1])
            + (inverse[r][2] * rows[2] + inverse[r][3] * rows[3])
            for r in range(4)
        ]
        for t in range(6):
            old = tiles[t]
            cols = [
                jnp.broadcast_to(old[:, first + c : first + c + 1], (8, 128))
                for c in range(4)
            ]
            change = (cols[0] * scaled[0] + cols[1] * scaled[1]) + (
                cols[2] * scaled[2] + cols[3] * scaled[3]
            )
            new = jnp.where(inside, 0.0, old) - change
            if t == home:
                for r in range(4):
                    new = jnp.where(row == place + r, -scaled[r], new)
            tiles[t] = new
    return tiles


def unpack(low, high):
    lane = lanes((8, 128))
    row = lax.broadcasted_iota(jnp.int32, (8, 128), 0)
    tiles = [low, high]
    tiles += [pltpu.roll(x, 96, 1) for x in (low, high)]
    tiles += [pltpu.roll(x, 80, 1) for x in (low, high)]
    full = jnp.concatenate(tiles, axis=0)
    keep = lanes((SIDE, 128)) // 16 >= lax.broadcasted_iota(jnp.int32, (SIDE, 128), 0) // 16
    upper = jnp.where(keep & (lanes((SIDE, 128)) < SIDE), full, 0.0)
    square = jnp.concatenate([upper, jnp.zeros((128 - SIDE, 128), F32)], axis=0)
    flipped = square.T[:SIDE]
    full = jnp.where(keep, upper, flipped)
    tiles = [full[8 * t : 8 * t + 8] for t in range(6)]
    tiles[5] = jnp.where((row == 3) & (lane == NB), 1.0, tiles[5])
    return tiles


def kernel(
    visits,
    patches,
    template_ref,
    across_ref,
    down_ref,
    weight_ref,
    patch_ref,
    science_ref,
    coef_ref,
    residual_ref,
    template_own,
    across_own,
    down_own,
    weight_own,
    patch_own,
    across_scr,
    down_scr,
    turn_scr,
    choice_scr,
    w_own,
    rows_scr,
    wide_scr,
    image_scr,
    sci_recv,
    sci_scr,
    w_recv,
    gram_scr,
    gram_pair,
    side_msg,
    side_near,
    near_msg,
    near_inbox,
    coef_row,
    coef_box,
    own_sem,
    small_sem,
    sci_send,
    sci_sem,
    w_send,
    w_sem,
    msg_send,
    msg_sem,
    near_send,
    near_sem,
    near_side_send,
    near_side_sem,
    row_send,
    row_sem,
):
    me_v = lax.axis_index("visit")
    me_q = lax.axis_index("patch")
    barrier = pltpu.get_barrier_semaphore()

    def visit_peer(step):
        return lax.rem(me_v + step, visits), me_q

    def patch_peer(step):
        return me_v, lax.rem(me_q + step + patches, patches)

    side_v = lax.rem(me_v, 2)
    chip = lax.div(me_v, 2)
    partner = (me_v + 1 - 2 * side_v, me_q)

    def rank(v):
        return 4 * lax.rem(v, 2) + lax.div(v, 2)

    others = range(1, 8)
    around = (-2, -1, 1, 2)

    order = (4, 3, 5, 2, 6, 1, 7)
    for peer in [visit_peer(j) for j in order] + [patch_peer(j) for j in around]:
        pl.semaphore_signal(barrier, inc=1, device_id=peer, device_id_type=MESH)

    small = [
        pltpu.make_async_copy(source, target, small_sem.at[n])
        for n, (source, target) in enumerate(
            (
                (weight_ref, weight_own),
                (across_ref, across_own),
                (down_ref, down_own),
                (patch_ref, patch_own),
                (template_ref, template_own),
            )
        )
    ]
    for copy in small:
        copy.start()

    own_copy = pltpu.make_async_copy(science_ref.at[0, 0, me_v], sci_recv.at[rank(me_v)], own_sem)
    own_copy.start()
    for copy in small:
        copy.wait()
    w_own[...] = jnp.concatenate(
        [weight_own[0, 0].astype(F32), jnp.zeros((8, 112), F32)], axis=1
    )
    for c in range(2):
        w_recv[pl.ds(2 * rank(me_v) + c, 1), :] = w_own[pl.ds(2 * chip + c, 1), :]
    tap = lax.broadcasted_iota(jnp.int32, (TAPS, 128), 0)
    column = lanes((TAPS, 128)) % STAMP
    backwards = ((column + tap) % STAMP == 0).astype(F32).astype(BF16)
    forwards = (column == tap).astype(F32).astype(BF16)
    nothing5 = jnp.zeros((5, 128), F32)
    across_scr[NB:, :] = nothing5
    first_axes = (((0,), (0,)), ((), ()))
    across_scr[0:NB, :] = lax.dot_general(
        across_own[...].astype(BF16), backwards, first_axes, preferred_element_type=F32
    )
    down_scr[NB:, :] = nothing5
    down_scr[0:NB, :] = lax.dot_general(
        down_own[...].astype(BF16), forwards, first_axes, preferred_element_type=F32
    )
    near = jnp.concatenate([patch_own[0], jnp.zeros((1, 112), jnp.int32)], axis=1)
    near = lax.rem(near - me_q + 1 + patches, patches).astype(F32)
    near16 = jnp.broadcast_to(near, (16, 128))
    diagonal = lanes((16, 128)) == lax.broadcasted_iota(jnp.int32, (16, 128), 0)
    choice_scr[...] = jnp.broadcast_to(
        jnp.sum(jnp.where(diagonal, near16, 0.0), axis=1, keepdims=True), (16, 128)
    )
    flat = template_own[0, 0].astype(F32)
    for z in range(SIDE):
        turn_scr[16 * z : 16 * z + 16, 0:SIDE] = flat[:, SIDE * z : SIDE * z + SIDE]
    stamps = jnp.concatenate(
        [
            jnp.concatenate(
                [
                    turn_scr[pl.ds(4 * g + s, SIDE, stride=16), :][:, :SIDE]
                    for s in range(4)
                ],
                axis=1,
            )
            for g in range(4)
        ],
        axis=0,
    ).astype(BF16)
    pl.semaphore_wait(barrier, len(others) + len(around))

    def send(source, target, sems, peer):
        pltpu.make_async_remote_copy(
            src_ref=source,
            dst_ref=target,
            send_sem=sems[0],
            recv_sem=sems[1],
            device_id=peer,
            device_id_type=MESH,
        ).start()

    def wait(like, sem):
        pltpu.make_async_copy(like, like, sem).wait()

    for j in order:
        peer = visit_peer(j)
        send(
            w_own.at[pl.ds(2 * lax.div(peer[0], 2), 2), :],
            w_recv.at[pl.ds(2 * rank(me_v), 2), :],
            (w_send, w_sem),
            peer,
        )
    for j in order:
        peer = visit_peer(j)
        send(
            science_ref.at[0, 0, peer[0]],
            sci_recv.at[rank(me_v)],
            (sci_send, sci_sem),
            peer,
        )

    shape = (SIDE, 128)
    past = lax.broadcasted_iota(jnp.int32, shape, 0) - lanes(shape) % STAMP
    band = (past >= 0) & (past < TAPS)
    masks = [
        (band & (lanes(shape) // STAMP == s)).astype(F32).astype(BF16) for s in range(4)
    ]
    rows_scr[44:48] = jnp.zeros((4, SIDE, 512), BF16)

    @pl.loop(0, 22, unroll=22)
    def make_rows(pair):
        right = []
        for j in range(2):
            taps = across_scr[pl.ds(2 * pair + j, 1), :]
            table = pltpu.roll(
                jnp.broadcast_to(taps, (STAMP, 128)), 0, 1, stride=1, stride_axis=0
            )
            table = jnp.concatenate([table, table[: SIDE - STAMP]], axis=0).astype(BF16)
            right.append(jnp.concatenate([table * m for m in masks], axis=0))
        right = jnp.concatenate(right, axis=1)
        out = jnp.dot(stamps, right, preferred_element_type=F32).astype(BF16)
        for j in range(2):
            for g in range(4):
                rows_scr[2 * pair + j, :, 128 * g : 128 * g + 128] = out[
                    SIDE * g : SIDE * g + SIDE, 128 * j : 128 * j + 128
                ]

    within = lanes((8, 128)) // STAMP - lax.broadcasted_iota(jnp.int32, (8, 128), 0)
    owner, owner4 = within == 0, within == -4

    @pl.loop(0, 6, unroll=6)
    def make_images(group):
        first = pl.multiple_of(group * 8, 8)
        taps = down_scr[pl.ds(first, 8), :]
        left = jnp.concatenate(
            [jnp.where(owner, taps, 0.0), jnp.where(owner4, taps, 0.0)], axis=1
        )
        left = jnp.concatenate(
            [left]
            + [
                jnp.concatenate(
                    [
                        pltpu.roll(left[:, :128], y, 1),
                        pltpu.roll(left[:, 128:], y, 1),
                    ],
                    axis=1,
                )
                for y in range(1, 16)
            ],
            axis=0,
        ).astype(BF16)
        for half in range(2):
            right = rows_scr[pl.ds(first, 8), 16 * half : 16 * half + 32, :]
            out = jnp.dot(left, right.reshape(256, 512), preferred_element_type=F32)
            wide_scr[16 * half : 16 * half + 16, pl.ds(first, 8), :] = out.reshape(16, 8, 512)

    lane = lanes((SIDE, 128))
    even = lane // STAMP % 2 == 0
    lower = lane < 64

    @pl.loop(0, 8, unroll=8)
    def regroup(quad):
        for g in range(4):
            part = [
                wide_scr[4 * quad + r, :, 128 * g : 128 * g + 128] for r in range(4)
            ]
            for a, b in ((0, 1), (2, 3)):
                x, y = part[a], part[b]
                part[a] = jnp.where(even, x, pltpu.roll(y, 32, 1))
                part[b] = jnp.where(even, pltpu.roll(x, 96, 1), y)
            for a, b in ((0, 2), (1, 3)):
                x, y = part[a], part[b]
                part[a] = jnp.where(lower, x, pltpu.roll(y, 64, 1))
                part[b] = jnp.where(lower, pltpu.roll(x, 64, 1), y)
            for s in range(4):
                image_scr[4 * g + s, :, pl.ds(pl.multiple_of(quad * 128, 128), 128)] = part[
                    s
                ].astype(BF16)

    lane16 = lanes((16, 128))
    second_axes = (((1,), (1,)), ((), ()))

    @pl.loop(0, 16, unroll=16)
    def make_grams(s):
        image = image_scr[s]
        out = lax.dot_general(image, image, second_axes, preferred_element_type=F32)
        out = jnp.concatenate([out, jnp.zeros((SIDE, 80), F32)], axis=1)
        packed = jnp.where(
            lane16 < 48,
            out[0:16],
            jnp.where(
                lane16 < 80,
                pltpu.roll(out[16:32], 32, 1),
                pltpu.roll(out[32:48], 48, 1),
            ),
        )
        gram_scr[pl.ds(pl.multiple_of(s * 16, 16), 16), :] = packed

    gram_scr[256:264, :] = near16[0:8]
    send(gram_scr, gram_pair, (msg_send, msg_sem), partner)

    def split(source):
        full = jnp.concatenate(
            [source[pl.ds(r, 16, stride=16), :] for r in range(16)], axis=1
        )
        top = full.astype(BF16)
        rest = full - top.astype(F32)
        middle = rest.astype(BF16)
        return [top, middle, (rest - middle.astype(F32)).astype(BF16)]

    right = split(gram_scr)
    wait(gram_pair, msg_sem)
    right = jnp.concatenate(right + split(gram_pair), axis=0)
    wait(w_recv.at[2:], w_sem)
    even_core = lanes((8, 128)) >= 128 * side_v
    by_core = [w_recv[pl.ds(c, 8, stride=2), :] for c in range(2)]
    weights = jnp.where(even_core, by_core[0], by_core[1])
    offset = near16[0:8]
    weighted = [jnp.where(offset == float(o), weights, 0.0) for o in range(REACH)]
    theirs = jnp.where(even_core, by_core[1], by_core[0])
    offset = gram_pair[256:264, :]
    both = [weighted, [jnp.where(offset == float(o), theirs, 0.0) for o in range(REACH)]]
    left = []
    for rows in both:
        half = jnp.concatenate(
            [jnp.where(even_core[:4], x[:4], x[4:]) for x in rows], axis=0
        )
        left += [half[:, :16].astype(BF16)] * 3
    systems = jnp.dot(
        jnp.concatenate(left, axis=1), right, preferred_element_type=F32
    )
    for r in range(16):
        for o in range(REACH):
            near_msg[pl.ds(16 * o + r, 4, stride=64), :] = systems[
                4 * o : 4 * o + 4, 128 * r : 128 * r + 128
            ]

    near = [(o, j) for o in range(REACH) for j in range(4) if (o, j) != (1, 0)]
    near.sort(key=lambda t: -abs(t[0] - 1) - min(t[1], 4 - t[1]))
    for o, j in near:
        there = lax.rem(chip + j, 4)
        send(
            near_msg.at[pl.ds(pl.multiple_of(64 * there + 16 * o, 16), 16), :],
            near_inbox.at[4 * o + j],
            (near_send, near_sem),
            (2 * there + side_v, patch_peer(o - 1)[1]),
        )

    own_copy.wait()
    wait(sci_recv.at[1:], sci_sem)
    for v in range(8):
        for t in range(8):
            sci_scr[128 * t + 16 * v : 128 * t + 16 * v + 16, :] = sci_recv[
                v, :, 128 * t : 128 * t + 128
            ].astype(F32)

    def exposures(s):
        return [sci_scr[pl.ds(128 * t + s, 8, stride=16), :] for t in range(8)]

    sides = [jnp.zeros((8, SIDE), F32) for _ in range(REACH)]
    for s in range(16):
        science = jnp.concatenate(exposures(s), axis=1).astype(BF16)
        out = lax.dot_general(
            science, image_scr[s], second_axes, preferred_element_type=F32
        )
        for o in range(REACH):
            factor = jnp.broadcast_to(weighted[o][:, s : s + 1], (8, SIDE))
            sides[o] = sides[o] + factor * out
    for o in range(REACH):
        side_msg[pl.ds(o, 8, stride=8), :] = jnp.concatenate(
            [sides[o], jnp.zeros((8, 80), F32)], axis=1
        )
        side_msg[pl.ds(4 + o, 8, stride=8), :] = jnp.zeros((8, 128), F32)
    every = [(o, j) for o in range(REACH) for j in range(8) if (o, j) != (1, 0)]
    every.sort(key=lambda t: -abs(t[0] - 1) - (min(t[1], 8 - t[1]) + 1) // 2)
    for o, j in every:
        v = visit_peer(j)[0]
        send(
            side_msg.at[pl.ds(8 * rank(v) + o, 1), :],
            side_near.at[pl.ds(8 * o + j, 1), :],
            (near_side_send, near_side_sem),
            (v, patch_peer(o - 1)[1]),
        )

    total = near_msg[pl.ds(pl.multiple_of(64 * chip + 16, 16), 16), :]
    wait(near_inbox.at[1:], near_sem)
    for o, j in near:
        total = total + near_inbox[4 * o + j]
    inverse = invert(unpack(total[0:8], total[8:16]))
    side_near[8:9, :] = side_msg[pl.ds(8 * rank(me_v) + 1, 1), :]
    wait(near_msg.at[0:31, :], near_side_sem)
    side = jnp.sum(side_near[...], axis=0, keepdims=True)
    side = jnp.where(lanes((1, 128)) < NB, side, 0.0)
    side = jnp.broadcast_to(side, (8, 128))
    across = lanes((8, 128)) - lax.broadcasted_iota(jnp.int32, (8, 128), 0)
    answer = jnp.zeros((8, 128), F32)
    for t in range(6):
        value = jnp.sum(inverse[t] * side, axis=1, keepdims=True)
        answer = answer + jnp.where(across == 8 * t, value, 0.0)
    answer = jnp.sum(answer, axis=0, keepdims=True)
    answer = jnp.where(lanes((1, 128)) < NB, answer, 0.0)
    coef_row[...] = answer
    place = pl.ds(rank(me_v), 1)
    for o, j in every:
        send(
            coef_row,
            coef_box.at[o, place, :],
            (row_send, row_sem),
            (visit_peer(j)[0], patch_peer(1 - o)[1]),
        )
    coef_ref[0] = answer[:, :NB]
    coef_box[1, place, :] = answer
    wait(near_msg.at[0:31, :], row_sem)

    lane8 = lanes((8, 128))

    def fit(s, held):
        choice = jnp.broadcast_to(choice_scr[pl.ds(s, 1), :], (8, 128))
        coefs = coef_box[0]
        for o in range(1, REACH):
            coefs = jnp.where(choice == float(o), coef_box[o], coefs)
        model = jnp.dot(
            coefs[:, :SIDE].astype(BF16), image_scr[s], preferred_element_type=F32
        )
        diff = jnp.concatenate(exposures(s), axis=1) - model
        square = diff * diff
        part = square[:, 0:128]
        for t in range(1, 8):
            part = part + square[:, 128 * t : 128 * t + 128]
        return jnp.where(lane8 == s, jnp.sum(part, axis=1, keepdims=True), held)

    held = lax.fori_loop(0, 16, fit, jnp.zeros((8, 128), F32), unroll=16)
    held = held * weights * (1.0 / 1024.0)
    for v in range(8):
        row = 4 * (v % 2) + v // 2
        residual_ref[v, 0] = held[row : row + 1, :16]

    wait(w_recv.at[2:], w_send)
    wait(sci_recv.at[1:], sci_send)
    wait(gram_pair, msg_send)
    wait(near_inbox.at[1:], near_send)
    wait(near_msg.at[0:31, :], near_side_send)
    wait(near_msg.at[0:31, :], row_send)


def on_device(template, science, weight, stamp_patch, basis_across, basis_down):
    visits = lax.axis_size("visit")
    patches = lax.axis_size("patch")
    vmem = pl.BlockSpec(memory_space=pltpu.VMEM)
    dma = pltpu.SemaphoreType.DMA
    return pl.pallas_call(
        functools.partial(kernel, visits, patches),
        out_shape=(
            jax.ShapeDtypeStruct((1, 1, NB), F32),
            jax.ShapeDtypeStruct((8, 1, 1, 16), F32),
        ),
        in_specs=[pl.BlockSpec(memory_space=pltpu.HBM)] * 6,
        out_specs=(vmem, vmem),
        scratch_shapes=[
            pltpu.VMEM(template.shape, BF16),
            pltpu.VMEM((TAPS, NB), F32),
            pltpu.VMEM((TAPS, NB), F32),
            pltpu.VMEM(weight.shape, BF16),
            pltpu.VMEM(stamp_patch.shape, jnp.int32),
            pltpu.VMEM((SIDE, 128), F32),
            pltpu.VMEM((SIDE, 128), F32),
            pltpu.VMEM((SIDE * 16, 128), F32),
            pltpu.VMEM((16, 128), F32),
            pltpu.VMEM((8, 128), F32),
            pltpu.VMEM((48, SIDE, 512), BF16),
            pltpu.VMEM((STAMP, SIDE, 512), F32),
            pltpu.VMEM((16, SIDE, 1024), BF16),
            pltpu.VMEM((8, 16, 1024), BF16),
            pltpu.VMEM((1024, 128), F32),
            pltpu.VMEM((16, 128), F32),
            pltpu.VMEM((264, 128), F32),
            pltpu.VMEM((264, 128), F32),
            pltpu.VMEM((64, 128), F32),
            pltpu.VMEM((32, 128), F32),
            pltpu.VMEM((256, 128), F32),
            pltpu.VMEM((16, 16, 128), F32),
            pltpu.VMEM((1, 128), F32),
            pltpu.VMEM((REACH, 8, 128), F32),
        ]
        + [dma, dma((5,))] + [dma] * 12,
        compiler_params=pltpu.CompilerParams(
            collective_id=0, has_side_effects=True, vmem_limit_bytes=32 * 1024 * 1024
        ),
    )(
        *(
            pltpu.with_memory_space_constraint(x, pltpu.HBM)
            for x in (template, basis_across.T, basis_down.T, weight, stamp_patch, science)
        )
    )


def solution(mesh):
    return jax.shard_map(
        on_device,
        mesh=mesh,
        in_specs=(
            P("patch", "visit", None, None),
            P("visit", "patch", None, None, None),
            P("visit", "patch", None, None),
            P("patch", "visit", None),
            P(),
            P(),
        ),
        out_specs=(P("visit", "patch", None), P(None, "patch", "visit", None)),
        check_vma=False,
    )
```

```python
import functools

import jax
import jax.numpy as jnp
from jax import lax
from jax.experimental import pallas as pl
from jax.experimental.pallas import tpu as pltpu
from jax.sharding import PartitionSpec as P

MESH = pl.DeviceIdType.MESH
F32 = jnp.float32
BF16 = jnp.bfloat16

STAMP = 32
TAPS = 17
SIDE = 48
NB = 43
REACH = 4


def lanes(shape):
    return lax.broadcasted_iota(jnp.int32, shape, len(shape) - 1)


def inverse_4x4(m):
    p, q, s = m[0][0], m[0][1], m[1][1]
    i = 1.0 / (p * s - q * q)
    a, b, c = s * i, -q * i, p * i
    e, f, g, h = m[0][2], m[0][3], m[1][2], m[1][3]
    ae, af = a * e + b * g, a * f + b * h
    ce, cf = b * e + c * g, b * f + c * h
    t = m[2][2] - (e * ae + g * ce)
    u = m[2][3] - (e * af + g * cf)
    w = m[3][3] - (f * af + h * cf)
    j = 1.0 / (t * w - u * u)
    x, y, z = w * j, -u * j, t * j
    r00, r01 = -(ae * x + af * y), -(ae * y + af * z)
    r10, r11 = -(ce * x + cf * y), -(ce * y + cf * z)
    n00 = a - (r00 * ae + r01 * af)
    n01 = b - (r00 * ce + r01 * cf)
    n11 = c - (r10 * ce + r11 * cf)
    return (
        (n00, n01, r00, r01),
        (n01, n11, r10, r11),
        (r00, r10, x, y),
        (r01, r11, y, z),
    )


def invert(tiles):
    lane = lanes((8, 128))
    row = lax.broadcasted_iota(jnp.int32, (8, 128), 0)
    tiles = list(tiles)
    for block in range(11):
        first = 4 * block
        home, place = first // 8, first % 8
        rows = [
            jnp.broadcast_to(tiles[home][place + c : place + c + 1, :], (8, 128))
            for c in range(4)
        ]
        pivot = [[None] * 4 for _ in range(4)]
        for r in range(4):
            for c in range(r, 4):
                value = jnp.broadcast_to(rows[r][:, first + c : first + c + 1], (8, 128))
                pivot[r][c] = pivot[c][r] = value
        inverse = inverse_4x4(pivot)
        inside = (lane >= first) & (lane < first + 4)
        rows = [
            jnp.where(inside, jnp.where(lane == first + c, -1.0, 0.0), rows[c])
            for c in range(4)
        ]
        scaled = [
            (inverse[r][0] * rows[0] + inverse[r][1] * rows[1])
            + (inverse[r][2] * rows[2] + inverse[r][3] * rows[3])
            for r in range(4)
        ]
        for t in range(6):
            old = tiles[t]
            cols = [
                jnp.broadcast_to(old[:, first + c : first + c + 1], (8, 128))
                for c in range(4)
            ]
            change = (cols[0] * scaled[0] + cols[1] * scaled[1]) + (
                cols[2] * scaled[2] + cols[3] * scaled[3]
            )
            new = jnp.where(inside, 0.0, old) - change
            if t == home:
                for r in range(4):
                    new = jnp.where(row == place + r, -scaled[r], new)
            tiles[t] = new
    return tiles


def unpack(low, high):
    lane = lanes((8, 128))
    row = lax.broadcasted_iota(jnp.int32, (8, 128), 0)
    tiles = [low, high]
    tiles += [pltpu.roll(x, 96, 1) for x in (low, high)]
    tiles += [pltpu.roll(x, 80, 1) for x in (low, high)]
    full = jnp.concatenate(tiles, axis=0)
    keep = lanes((SIDE, 128)) // 16 >= lax.broadcasted_iota(jnp.int32, (SIDE, 128), 0) // 16
    upper = jnp.where(keep & (lanes((SIDE, 128)) < SIDE), full, 0.0)
    square = jnp.concatenate([upper, jnp.zeros((128 - SIDE, 128), F32)], axis=0)
    flipped = square.T[:SIDE]
    full = jnp.where(keep, upper, flipped)
    tiles = [full[8 * t : 8 * t + 8] for t in range(6)]
    tiles[5] = jnp.where((row == 3) & (lane == NB), 1.0, tiles[5])
    return tiles


def kernel(
    visits,
    patches,
    template_ref,
    across_ref,
    down_ref,
    weight_ref,
    patch_ref,
    science_ref,
    coef_ref,
    residual_ref,
    template_own,
    across_own,
    down_own,
    weight_own,
    patch_own,
    across_scr,
    down_scr,
    turn_scr,
    choice_scr,
    w_own,
    rows_scr,
    wide_scr,
    image_scr,
    sci_recv,
    sci_scr,
    w_recv,
    gram_scr,
    gram_pair,
    side_msg,
    side_near,
    near_msg,
    near_inbox,
    coef_row,
    coef_box,
    own_sem,
    small_sem,
    sci_send,
    sci_sem,
    w_send,
    w_sem,
    msg_send,
    msg_sem,
    near_send,
    near_sem,
    near_side_send,
    near_side_sem,
    row_send,
    row_sem,
):
    me_v = lax.axis_index("visit")
    me_q = lax.axis_index("patch")
    barrier = pltpu.get_barrier_semaphore()

    def visit_peer(step):
        return lax.rem(me_v + step, visits), me_q

    def patch_peer(step):
        return me_v, lax.rem(me_q + step + patches, patches)

    side_v = lax.rem(me_v, 2)
    chip = lax.div(me_v, 2)
    partner = (me_v + 1 - 2 * side_v, me_q)

    def rank(v):
        return 4 * lax.rem(v, 2) + lax.div(v, 2)

    others = range(1, 8)
    around = (-2, -1, 1, 2)

    order = (4, 3, 5, 2, 6, 1, 7)
    for peer in [visit_peer(j) for j in order] + [patch_peer(j) for j in around]:
        pl.semaphore_signal(barrier, inc=1, device_id=peer, device_id_type=MESH)

    small = [
        pltpu.make_async_copy(source, target, small_sem.at[n])
        for n, (source, target) in enumerate(
            (
                (weight_ref, weight_own),
                (across_ref, across_own),
                (down_ref, down_own),
                (patch_ref, patch_own),
                (template_ref, template_own),
            )
        )
    ]
    for copy in small:
        copy.start()

    own_copy = pltpu.make_async_copy(science_ref.at[0, 0, me_v], sci_recv.at[rank(me_v)], own_sem)
    own_copy.start()
    for copy in small:
        copy.wait()
    w_own[...] = jnp.concatenate(
        [weight_own[0, 0].astype(F32), jnp.zeros((8, 112), F32)], axis=1
    )
    for c in range(2):
        w_recv[pl.ds(2 * rank(me_v) + c, 1), :] = w_own[pl.ds(2 * chip + c, 1), :]
    tap = lax.broadcasted_iota(jnp.int32, (TAPS, 128), 0)
    column = lanes((TAPS, 128)) % STAMP
    backwards = ((column + tap) % STAMP == 0).astype(F32).astype(BF16)
    forwards = (column == tap).astype(F32).astype(BF16)
    nothing5 = jnp.zeros((5, 128), F32)
    across_scr[NB:, :] = nothing5
    first_axes = (((0,), (0,)), ((), ()))
    across_scr[0:NB, :] = lax.dot_general(
        across_own[...].astype(BF16), backwards, first_axes, preferred_element_type=F32
    )
    down_scr[NB:, :] = nothing5
    down_scr[0:NB, :] = lax.dot_general(
        down_own[...].astype(BF16), forwards, first_axes, preferred_element_type=F32
    )
    near = jnp.concatenate([patch_own[0], jnp.zeros((1, 112), jnp.int32)], axis=1)
    near = lax.rem(near - me_q + 1 + patches, patches).astype(F32)
    near16 = jnp.broadcast_to(near, (16, 128))
    diagonal = lanes((16, 128)) == lax.broadcasted_iota(jnp.int32, (16, 128), 0)
    choice_scr[...] = jnp.broadcast_to(
        jnp.sum(jnp.where(diagonal, near16, 0.0), axis=1, keepdims=True), (16, 128)
    )
    flat = template_own[0, 0].astype(F32)
    for z in range(SIDE):
        turn_scr[16 * z : 16 * z + 16, 0:SIDE] = flat[:, SIDE * z : SIDE * z + SIDE]
    stamps = jnp.concatenate(
        [
            jnp.concatenate(
                [
                    turn_scr[pl.ds(4 * g + s, SIDE, stride=16), :][:, :SIDE]
                    for s in range(4)
                ],
                axis=1,
            )
            for g in range(4)
        ],
        axis=0,
    ).astype(BF16)
    def send(source, target, sems, peer):
        pltpu.make_async_remote_copy(
            src_ref=source,
            dst_ref=target,
            send_sem=sems[0],
            recv_sem=sems[1],
            device_id=peer,
            device_id_type=MESH,
        ).start()

    def wait(like, sem):
        pltpu.make_async_copy(like, like, sem).wait()

    shape = (SIDE, 128)
    past = lax.broadcasted_iota(jnp.int32, shape, 0) - lanes(shape) % STAMP
    band = (past >= 0) & (past < TAPS)
    masks = [
        (band & (lanes(shape) // STAMP == s)).astype(F32).astype(BF16) for s in range(4)
    ]
    rows_scr[44:48] = jnp.zeros((4, SIDE, 512), BF16)

    @pl.loop(0, 22, unroll=22)
    def make_rows(pair):
        right = []
        for j in range(2):
            taps = across_scr[pl.ds(2 * pair + j, 1), :]
            table = pltpu.roll(
                jnp.broadcast_to(taps, (STAMP, 128)), 0, 1, stride=1, stride_axis=0
            )
            table = jnp.concatenate([table, table[: SIDE - STAMP]], axis=0).astype(BF16)
            right.append(jnp.concatenate([table * m for m in masks], axis=0))
        right = jnp.concatenate(right, axis=1)
        out = jnp.dot(stamps, right, preferred_element_type=F32).astype(BF16)
        for j in range(2):
            for g in range(4):
                rows_scr[2 * pair + j, :, 128 * g : 128 * g + 128] = out[
                    SIDE * g : SIDE * g + SIDE, 128 * j : 128 * j + 128
                ]

    pl.semaphore_wait(barrier, len(others) + len(around))

    for j in order:
        peer = visit_peer(j)
        send(
            w_own.at[pl.ds(2 * lax.div(peer[0], 2), 2), :],
            w_recv.at[pl.ds(2 * rank(me_v), 2), :],
            (w_send, w_sem),
            peer,
        )
    for j in order:
        peer = visit_peer(j)
        send(
            science_ref.at[0, 0, peer[0]],
            sci_recv.at[rank(me_v)],
            (sci_send, sci_sem),
            peer,
        )

    within = lanes((8, 128)) // STAMP - lax.broadcasted_iota(jnp.int32, (8, 128), 0)
    owner, owner4 = within == 0, within == -4

    @pl.loop(0, 6, unroll=6)
    def make_images(group):
        first = pl.multiple_of(group * 8, 8)
        taps = down_scr[pl.ds(first, 8), :]
        left = jnp.concatenate(
            [jnp.where(owner, taps, 0.0), jnp.where(owner4, taps, 0.0)], axis=1
        )
        left = jnp.concatenate(
            [left]
            + [
                jnp.concatenate(
                    [
                        pltpu.roll(left[:, :128], y, 1),
                        pltpu.roll(left[:, 128:], y, 1),
                    ],
                    axis=1,
                )
                for y in range(1, 16)
            ],
            axis=0,
        ).astype(BF16)
        for half in range(2):
            right = rows_scr[pl.ds(first, 8), 16 * half : 16 * half + 32, :]
            out = jnp.dot(left, right.reshape(256, 512), preferred_element_type=F32)
            wide_scr[16 * half : 16 * half + 16, pl.ds(first, 8), :] = out.reshape(16, 8, 512)

    lane = lanes((SIDE, 128))
    even = lane // STAMP % 2 == 0
    lower = lane < 64

    @pl.loop(0, 8, unroll=8)
    def regroup(quad):
        for g in range(4):
            part = [
                wide_scr[4 * quad + r, :, 128 * g : 128 * g + 128] for r in range(4)
            ]
            for a, b in ((0, 1), (2, 3)):
                x, y = part[a], part[b]
                part[a] = jnp.where(even, x, pltpu.roll(y, 32, 1))
                part[b] = jnp.where(even, pltpu.roll(x, 96, 1), y)
            for a, b in ((0, 2), (1, 3)):
                x, y = part[a], part[b]
                part[a] = jnp.where(lower, x, pltpu.roll(y, 64, 1))
                part[b] = jnp.where(lower, pltpu.roll(x, 64, 1), y)
            for s in range(4):
                image_scr[4 * g + s, :, pl.ds(pl.multiple_of(quad * 128, 128), 128)] = part[
                    s
                ].astype(BF16)

    lane16 = lanes((16, 128))
    second_axes = (((1,), (1,)), ((), ()))

    def make_gram(s):
        image = image_scr[s]
        out = lax.dot_general(image, image, second_axes, preferred_element_type=F32)
        out = jnp.concatenate([out, jnp.zeros((SIDE, 80), F32)], axis=1)
        packed = jnp.where(
            lane16 < 48,
            out[0:16],
            jnp.where(
                lane16 < 80,
                pltpu.roll(out[16:32], 32, 1),
                pltpu.roll(out[32:48], 48, 1),
            ),
        )
        gram_scr[16 * s : 16 * s + 16, :] = packed

    gram_scr[256:264, :] = near16[0:8]
    for first, last in ((0, 6), (6, 11), (11, 16)):
        for s in range(first, last):
            make_gram(s)
        rows = pl.ds(16 * first, 16 * (last - first) + 8 * (last == 16))
        send(gram_scr.at[rows, :], gram_pair.at[rows, :], (msg_send, msg_sem), partner)

    def split(source):
        full = jnp.concatenate(
            [source[pl.ds(r, 16, stride=16), :] for r in range(16)], axis=1
        )
        top = full.astype(BF16)
        rest = full - top.astype(F32)
        middle = rest.astype(BF16)
        return [top, middle, (rest - middle.astype(F32)).astype(BF16)]

    right = split(gram_scr)
    wait(gram_pair, msg_sem)
    right = jnp.concatenate(right + split(gram_pair), axis=0)
    wait(w_recv.at[2:], w_sem)
    even_core = lanes((8, 128)) >= 128 * side_v
    by_core = [w_recv[pl.ds(c, 8, stride=2), :] for c in range(2)]
    weights = jnp.where(even_core, by_core[0], by_core[1])
    offset = near16[0:8]
    weighted = [jnp.where(offset == float(o), weights, 0.0) for o in range(REACH)]
    theirs = jnp.where(even_core, by_core[1], by_core[0])
    offset = gram_pair[256:264, :]
    both = [weighted, [jnp.where(offset == float(o), theirs, 0.0) for o in range(REACH)]]
    left = []
    for rows in both:
        half = jnp.concatenate(
            [jnp.where(even_core[:4], x[:4], x[4:]) for x in rows], axis=0
        )
        left += [half[:, :16].astype(BF16)] * 3
    systems = jnp.dot(
        jnp.concatenate(left, axis=1), right, preferred_element_type=F32
    )
    for r in range(16):
        for o in range(REACH):
            near_msg[pl.ds(16 * o + r, 4, stride=64), :] = systems[
                4 * o : 4 * o + 4, 128 * r : 128 * r + 128
            ]

    near = [(o, j) for o in range(REACH) for j in range(4) if (o, j) != (1, 0)]
    near.sort(key=lambda t: -abs(t[0] - 1) - min(t[1], 4 - t[1]))
    for o, j in near:
        there = lax.rem(chip + j, 4)
        send(
            near_msg.at[pl.ds(pl.multiple_of(64 * there + 16 * o, 16), 16), :],
            near_inbox.at[4 * o + j],
            (near_send, near_sem),
            (2 * there + side_v, patch_peer(o - 1)[1]),
        )

    own_copy.wait()
    wait(sci_recv.at[1:], sci_sem)
    for v in range(8):
        for t in range(8):
            sci_scr[128 * t + 16 * v : 128 * t + 16 * v + 16, :] = sci_recv[
                v, :, 128 * t : 128 * t + 128
            ].astype(F32)

    def exposures(s):
        return [sci_scr[pl.ds(128 * t + s, 8, stride=16), :] for t in range(8)]

    sides = [jnp.zeros((8, SIDE), F32) for _ in range(REACH)]
    for s in range(16):
        science = jnp.concatenate(exposures(s), axis=1).astype(BF16)
        out = lax.dot_general(
            science, image_scr[s], second_axes, preferred_element_type=F32
        )
        for o in range(REACH):
            factor = jnp.broadcast_to(weighted[o][:, s : s + 1], (8, SIDE))
            sides[o] = sides[o] + factor * out
    for o in range(REACH):
        side_msg[pl.ds(o, 8, stride=8), :] = jnp.concatenate(
            [sides[o], jnp.zeros((8, 80), F32)], axis=1
        )
        side_msg[pl.ds(4 + o, 8, stride=8), :] = jnp.zeros((8, 128), F32)
    every = [(o, j) for o in range(REACH) for j in range(8) if (o, j) != (1, 0)]
    every.sort(key=lambda t: -abs(t[0] - 1) - (min(t[1], 8 - t[1]) + 1) // 2)
    for o, j in every:
        v = visit_peer(j)[0]
        send(
            side_msg.at[pl.ds(8 * rank(v) + o, 1), :],
            side_near.at[pl.ds(8 * o + j, 1), :],
            (near_side_send, near_side_sem),
            (v, patch_peer(o - 1)[1]),
        )

    total = near_msg[pl.ds(pl.multiple_of(64 * chip + 16, 16), 16), :]
    wait(near_inbox.at[1:], near_sem)
    for o, j in near:
        total = total + near_inbox[4 * o + j]
    inverse = invert(unpack(total[0:8], total[8:16]))
    side_near[8:9, :] = side_msg[pl.ds(8 * rank(me_v) + 1, 1), :]
    wait(near_msg.at[0:31, :], near_side_sem)
    side = jnp.sum(side_near[...], axis=0, keepdims=True)
    side = jnp.where(lanes((1, 128)) < NB, side, 0.0)
    side = jnp.broadcast_to(side, (8, 128))
    across = lanes((8, 128)) - lax.broadcasted_iota(jnp.int32, (8, 128), 0)
    answer = jnp.zeros((8, 128), F32)
    for t in range(6):
        value = jnp.sum(inverse[t] * side, axis=1, keepdims=True)
        answer = answer + jnp.where(across == 8 * t, value, 0.0)
    answer = jnp.sum(answer, axis=0, keepdims=True)
    answer = jnp.where(lanes((1, 128)) < NB, answer, 0.0)
    coef_row[...] = answer
    place = pl.ds(rank(me_v), 1)
    for o, j in every:
        send(
            coef_row,
            coef_box.at[o, place, :],
            (row_send, row_sem),
            (visit_peer(j)[0], patch_peer(1 - o)[1]),
        )
    coef_ref[0] = answer[:, :NB]
    coef_box[1, place, :] = answer
    wait(near_msg.at[0:31, :], row_sem)

    lane8 = lanes((8, 128))

    def fit(s, held):
        choice = jnp.broadcast_to(choice_scr[pl.ds(s, 1), :], (8, 128))
        coefs = coef_box[0]
        for o in range(1, REACH):
            coefs = jnp.where(choice == float(o), coef_box[o], coefs)
        model = jnp.dot(
            coefs[:, :SIDE].astype(BF16), image_scr[s], preferred_element_type=F32
        )
        diff = jnp.concatenate(exposures(s), axis=1) - model
        square = diff * diff
        part = square[:, 0:128]
        for t in range(1, 8):
            part = part + square[:, 128 * t : 128 * t + 128]
        return jnp.where(lane8 == s, jnp.sum(part, axis=1, keepdims=True), held)

    held = lax.fori_loop(0, 16, fit, jnp.zeros((8, 128), F32), unroll=16)
    held = held * weights * (1.0 / 1024.0)
    for v in range(8):
        row = 4 * (v % 2) + v // 2
        residual_ref[v, 0] = held[row : row + 1, :16]

    wait(w_recv.at[2:], w_send)
    wait(sci_recv.at[1:], sci_send)
    wait(gram_pair, msg_send)
    wait(near_inbox.at[1:], near_send)
    wait(near_msg.at[0:31, :], near_side_send)
    wait(near_msg.at[0:31, :], row_send)


def hand_out(coef_ref, residual_ref, coef_out, residual_out, sems):
    copies = [
        pltpu.make_async_copy(coef_ref, coef_out, sems.at[0]),
        pltpu.make_async_copy(residual_ref, residual_out, sems.at[1]),
    ]
    for copy in copies:
        copy.start()
    for copy in copies:
        copy.wait()


def on_device(template, science, weight, stamp_patch, basis_across, basis_down):
    visits = lax.axis_size("visit")
    patches = lax.axis_size("patch")
    vmem = pl.BlockSpec(memory_space=pltpu.VMEM)
    dma = pltpu.SemaphoreType.DMA
    found = pl.pallas_call(
        functools.partial(kernel, visits, patches),
        out_shape=(
            jax.ShapeDtypeStruct((1, 1, NB), F32),
            jax.ShapeDtypeStruct((8, 1, 1, 16), F32),
        ),
        in_specs=[pl.BlockSpec(memory_space=pltpu.HBM)] * 6,
        out_specs=(vmem, vmem),
        scratch_shapes=[
            pltpu.VMEM(template.shape, BF16),
            pltpu.VMEM((TAPS, NB), F32),
            pltpu.VMEM((TAPS, NB), F32),
            pltpu.VMEM(weight.shape, BF16),
            pltpu.VMEM(stamp_patch.shape, jnp.int32),
            pltpu.VMEM((SIDE, 128), F32),
            pltpu.VMEM((SIDE, 128), F32),
            pltpu.VMEM((SIDE * 16, 128), F32),
            pltpu.VMEM((16, 128), F32),
            pltpu.VMEM((8, 128), F32),
            pltpu.VMEM((48, SIDE, 512), BF16),
            pltpu.VMEM((STAMP, SIDE, 512), F32),
            pltpu.VMEM((16, SIDE, 1024), BF16),
            pltpu.VMEM((8, 16, 1024), BF16),
            pltpu.VMEM((1024, 128), F32),
            pltpu.VMEM((16, 128), F32),
            pltpu.VMEM((264, 128), F32),
            pltpu.VMEM((264, 128), F32),
            pltpu.VMEM((64, 128), F32),
            pltpu.VMEM((32, 128), F32),
            pltpu.VMEM((256, 128), F32),
            pltpu.VMEM((16, 16, 128), F32),
            pltpu.VMEM((1, 128), F32),
            pltpu.VMEM((REACH, 8, 128), F32),
        ]
        + [dma, dma((5,))] + [dma] * 12,
        compiler_params=pltpu.CompilerParams(
            collective_id=0, has_side_effects=True, vmem_limit_bytes=32 * 1024 * 1024
        ),
    )(
        *(
            pltpu.with_memory_space_constraint(x, pltpu.HBM)
            for x in (template, basis_across.T, basis_down.T, weight, stamp_patch, science)
        )
    )
    return pl.pallas_call(
        hand_out,
        out_shape=(
            jax.ShapeDtypeStruct((1, 1, NB), F32),
            jax.ShapeDtypeStruct((8, 1, 1, 16), F32),
        ),
        in_specs=[vmem] * 2,
        out_specs=[pl.BlockSpec(memory_space=pl.ANY)] * 2,
        scratch_shapes=[dma((2,))],
    )(*(pltpu.with_memory_space_constraint(x, pltpu.VMEM) for x in found))


def solution(mesh):
    return jax.shard_map(
        on_device,
        mesh=mesh,
        in_specs=(
            P("patch", "visit", None, None),
            P("visit", "patch", None, None, None),
            P("visit", "patch", None, None),
            P("patch", "visit", None),
            P(),
            P(),
        ),
        out_specs=(P("visit", "patch", None), P(None, "patch", "visit", None)),
        check_vma=False,
    )
```

```python
import functools

import jax
import jax.numpy as jnp
from jax import lax
from jax.experimental import pallas as pl
from jax.experimental.pallas import tpu as pltpu
from jax.sharding import PartitionSpec as P

MESH = pl.DeviceIdType.MESH
F32 = jnp.float32
BF16 = jnp.bfloat16

STAMP = 32
TAPS = 17
SIDE = 48
NB = 43
REACH = 4


def lanes(shape):
    return lax.broadcasted_iota(jnp.int32, shape, len(shape) - 1)


def inverse_4x4(m):
    p, q, s = m[0][0], m[0][1], m[1][1]
    i = 1.0 / (p * s - q * q)
    a, b, c = s * i, -q * i, p * i
    e, f, g, h = m[0][2], m[0][3], m[1][2], m[1][3]
    ae, af = a * e + b * g, a * f + b * h
    ce, cf = b * e + c * g, b * f + c * h
    t = m[2][2] - (e * ae + g * ce)
    u = m[2][3] - (e * af + g * cf)
    w = m[3][3] - (f * af + h * cf)
    j = 1.0 / (t * w - u * u)
    x, y, z = w * j, -u * j, t * j
    r00, r01 = -(ae * x + af * y), -(ae * y + af * z)
    r10, r11 = -(ce * x + cf * y), -(ce * y + cf * z)
    n00 = a - (r00 * ae + r01 * af)
    n01 = b - (r00 * ce + r01 * cf)
    n11 = c - (r10 * ce + r11 * cf)
    return (
        (n00, n01, r00, r01),
        (n01, n11, r10, r11),
        (r00, r10, x, y),
        (r01, r11, y, z),
    )


def invert(tiles):
    lane = lanes((8, 128))
    row = lax.broadcasted_iota(jnp.int32, (8, 128), 0)
    tiles = list(tiles)
    for block in range(11):
        first = 4 * block
        home, place = first // 8, first % 8
        rows = [
            jnp.broadcast_to(tiles[home][place + c : place + c + 1, :], (8, 128))
            for c in range(4)
        ]
        pivot = [[None] * 4 for _ in range(4)]
        for r in range(4):
            for c in range(r, 4):
                value = jnp.broadcast_to(rows[r][:, first + c : first + c + 1], (8, 128))
                pivot[r][c] = pivot[c][r] = value
        inverse = inverse_4x4(pivot)
        inside = (lane >= first) & (lane < first + 4)
        rows = [
            jnp.where(inside, jnp.where(lane == first + c, -1.0, 0.0), rows[c])
            for c in range(4)
        ]
        scaled = [
            (inverse[r][0] * rows[0] + inverse[r][1] * rows[1])
            + (inverse[r][2] * rows[2] + inverse[r][3] * rows[3])
            for r in range(4)
        ]
        for t in range(6):
            old = tiles[t]
            cols = [
                jnp.broadcast_to(old[:, first + c : first + c + 1], (8, 128))
                for c in range(4)
            ]
            change = (cols[0] * scaled[0] + cols[1] * scaled[1]) + (
                cols[2] * scaled[2] + cols[3] * scaled[3]
            )
            new = jnp.where(inside, 0.0, old) - change
            if t == home:
                for r in range(4):
                    new = jnp.where(row == place + r, -scaled[r], new)
            tiles[t] = new
    return tiles


def unpack(low, high):
    lane = lanes((8, 128))
    row = lax.broadcasted_iota(jnp.int32, (8, 128), 0)
    tiles = [low, high]
    tiles += [pltpu.roll(x, 96, 1) for x in (low, high)]
    tiles += [pltpu.roll(x, 80, 1) for x in (low, high)]
    full = jnp.concatenate(tiles, axis=0)
    keep = lanes((SIDE, 128)) // 16 >= lax.broadcasted_iota(jnp.int32, (SIDE, 128), 0) // 16
    upper = jnp.where(keep & (lanes((SIDE, 128)) < SIDE), full, 0.0)
    square = jnp.concatenate([upper, jnp.zeros((128 - SIDE, 128), F32)], axis=0)
    flipped = square.T[:SIDE]
    full = jnp.where(keep, upper, flipped)
    tiles = [full[8 * t : 8 * t + 8] for t in range(6)]
    tiles[5] = jnp.where((row == 3) & (lane == NB), 1.0, tiles[5])
    return tiles


def kernel(
    visits,
    patches,
    template_ref,
    across_ref,
    down_ref,
    weight_ref,
    patch_ref,
    science_ref,
    coef_ref,
    residual_ref,
    template_own,
    across_own,
    down_own,
    weight_own,
    patch_own,
    across_scr,
    down_scr,
    turn_scr,
    choice_scr,
    w_own,
    rows_scr,
    wide_scr,
    image_scr,
    sci_recv,
    sci_scr,
    w_recv,
    gram_scr,
    gram_pair,
    side_msg,
    side_near,
    near_msg,
    near_inbox,
    coef_row,
    coef_box,
    own_sem,
    small_sem,
    sci_send,
    sci_sem,
    w_send,
    w_sem,
    msg_send,
    msg_sem,
    near_send,
    near_sem,
    near_side_send,
    near_side_sem,
    row_send,
    row_sem,
):
    me_v = lax.axis_index("visit")
    me_q = lax.axis_index("patch")
    barrier = pltpu.get_barrier_semaphore()

    def visit_peer(step):
        return lax.rem(me_v + step, visits), me_q

    def patch_peer(step):
        return me_v, lax.rem(me_q + step + patches, patches)

    side_v = lax.rem(me_v, 2)
    chip = lax.div(me_v, 2)
    partner = (me_v + 1 - 2 * side_v, me_q)

    def rank(v):
        return 4 * lax.rem(v, 2) + lax.div(v, 2)

    others = range(1, 8)
    around = (-2, -1, 1, 2)

    small = [
        pltpu.make_async_copy(source, target, small_sem.at[n])
        for n, (source, target) in enumerate(
            (
                (template_ref, template_own),
                (across_ref, across_own),
                (down_ref, down_own),
                (weight_ref, weight_own),
                (patch_ref, patch_own),
            )
        )
    ]
    for copy in small:
        copy.start()

    order = (4, 3, 5, 2, 6, 1, 7)
    for peer in [visit_peer(j) for j in order] + [patch_peer(j) for j in around]:
        pl.semaphore_signal(barrier, inc=1, device_id=peer, device_id_type=MESH)

    own_copy = pltpu.make_async_copy(science_ref.at[0, 0, me_v], sci_recv.at[rank(me_v)], own_sem)
    own_copy.start()
    small[0].wait()
    flat = template_own[0, 0].astype(F32)
    for z in range(SIDE):
        turn_scr[16 * z : 16 * z + 16, 0:SIDE] = flat[:, SIDE * z : SIDE * z + SIDE]
    stamps = jnp.concatenate(
        [
            jnp.concatenate(
                [
                    turn_scr[pl.ds(4 * g + s, SIDE, stride=16), :][:, :SIDE]
                    for s in range(4)
                ],
                axis=1,
            )
            for g in range(4)
        ],
        axis=0,
    ).astype(BF16)
    for copy in small[1:]:
        copy.wait()
    w_own[...] = jnp.concatenate(
        [weight_own[0, 0].astype(F32), jnp.zeros((8, 112), F32)], axis=1
    )
    for c in range(2):
        w_recv[pl.ds(2 * rank(me_v) + c, 1), :] = w_own[pl.ds(2 * chip + c, 1), :]
    tap = lax.broadcasted_iota(jnp.int32, (TAPS, 128), 0)
    column = lanes((TAPS, 128)) % STAMP
    backwards = ((column + tap) % STAMP == 0).astype(F32).astype(BF16)
    forwards = (column == tap).astype(F32).astype(BF16)
    nothing5 = jnp.zeros((5, 128), F32)
    across_scr[NB:, :] = nothing5
    first_axes = (((0,), (0,)), ((), ()))
    across_scr[0:NB, :] = lax.dot_general(
        across_own[...].astype(BF16), backwards, first_axes, preferred_element_type=F32
    )
    down_scr[NB:, :] = nothing5
    down_scr[0:NB, :] = lax.dot_general(
        down_own[...].astype(BF16), forwards, first_axes, preferred_element_type=F32
    )
    near = jnp.concatenate([patch_own[0], jnp.zeros((1, 112), jnp.int32)], axis=1)
    near = lax.rem(near - me_q + 1 + patches, patches).astype(F32)
    near16 = jnp.broadcast_to(near, (16, 128))
    diagonal = lanes((16, 128)) == lax.broadcasted_iota(jnp.int32, (16, 128), 0)
    choice_scr[...] = jnp.broadcast_to(
        jnp.sum(jnp.where(diagonal, near16, 0.0), axis=1, keepdims=True), (16, 128)
    )
    def send(source, target, sems, peer):
        pltpu.make_async_remote_copy(
            src_ref=source,
            dst_ref=target,
            send_sem=sems[0],
            recv_sem=sems[1],
            device_id=peer,
            device_id_type=MESH,
        ).start()

    def wait(like, sem):
        pltpu.make_async_copy(like, like, sem).wait()

    shape = (SIDE, 128)
    past = lax.broadcasted_iota(jnp.int32, shape, 0) - lanes(shape) % STAMP
    band = (past >= 0) & (past < TAPS)
    masks = [
        (band & (lanes(shape) // STAMP == s)).astype(F32).astype(BF16) for s in range(4)
    ]
    rows_scr[44:48] = jnp.zeros((4, SIDE, 512), BF16)

    @pl.loop(0, 22, unroll=22)
    def make_rows(pair):
        right = []
        for j in range(2):
            taps = across_scr[pl.ds(2 * pair + j, 1), :]
            table = pltpu.roll(
                jnp.broadcast_to(taps, (STAMP, 128)), 0, 1, stride=1, stride_axis=0
            )
            table = jnp.concatenate([table, table[: SIDE - STAMP]], axis=0).astype(BF16)
            right.append(jnp.concatenate([table * m for m in masks], axis=0))
        right = jnp.concatenate(right, axis=1)
        out = jnp.dot(stamps, right, preferred_element_type=F32).astype(BF16)
        for j in range(2):
            for g in range(4):
                rows_scr[2 * pair + j, :, 128 * g : 128 * g + 128] = out[
                    SIDE * g : SIDE * g + SIDE, 128 * j : 128 * j + 128
                ]

    pl.semaphore_wait(barrier, len(others) + len(around))

    for j in order:
        peer = visit_peer(j)
        send(
            w_own.at[pl.ds(2 * lax.div(peer[0], 2), 2), :],
            w_recv.at[pl.ds(2 * rank(me_v), 2), :],
            (w_send, w_sem),
            peer,
        )
    for j in order:
        peer = visit_peer(j)
        send(
            science_ref.at[0, 0, peer[0]],
            sci_recv.at[rank(me_v)],
            (sci_send, sci_sem),
            peer,
        )

    within = lanes((8, 128)) // STAMP - lax.broadcasted_iota(jnp.int32, (8, 128), 0)
    owner, owner4 = within == 0, within == -4

    @pl.loop(0, 6, unroll=6)
    def make_images(group):
        first = pl.multiple_of(group * 8, 8)
        taps = down_scr[pl.ds(first, 8), :]
        left = jnp.concatenate(
            [jnp.where(owner, taps, 0.0), jnp.where(owner4, taps, 0.0)], axis=1
        )
        left = jnp.concatenate(
            [left]
            + [
                jnp.concatenate(
                    [
                        pltpu.roll(left[:, :128], y, 1),
                        pltpu.roll(left[:, 128:], y, 1),
                    ],
                    axis=1,
                )
                for y in range(1, 16)
            ],
            axis=0,
        ).astype(BF16)
        for half in range(2):
            right = rows_scr[pl.ds(first, 8), 16 * half : 16 * half + 32, :]
            out = jnp.dot(left, right.reshape(256, 512), preferred_element_type=F32)
            wide_scr[16 * half : 16 * half + 16, pl.ds(first, 8), :] = out.reshape(16, 8, 512)

    lane = lanes((SIDE, 128))
    even = lane // STAMP % 2 == 0
    lower = lane < 64

    @pl.loop(0, 8, unroll=8)
    def regroup(quad):
        for g in range(4):
            part = [
                wide_scr[4 * quad + r, :, 128 * g : 128 * g + 128] for r in range(4)
            ]
            for a, b in ((0, 1), (2, 3)):
                x, y = part[a], part[b]
                part[a] = jnp.where(even, x, pltpu.roll(y, 32, 1))
                part[b] = jnp.where(even, pltpu.roll(x, 96, 1), y)
            for a, b in ((0, 2), (1, 3)):
                x, y = part[a], part[b]
                part[a] = jnp.where(lower, x, pltpu.roll(y, 64, 1))
                part[b] = jnp.where(lower, pltpu.roll(x, 64, 1), y)
            for s in range(4):
                image_scr[4 * g + s, :, pl.ds(pl.multiple_of(quad * 128, 128), 128)] = part[
                    s
                ].astype(BF16)

    lane16 = lanes((16, 128))
    second_axes = (((1,), (1,)), ((), ()))

    def make_gram(s):
        image = image_scr[s]
        out = lax.dot_general(image, image, second_axes, preferred_element_type=F32)
        out = jnp.concatenate([out, jnp.zeros((SIDE, 80), F32)], axis=1)
        packed = jnp.where(
            lane16 < 48,
            out[0:16],
            jnp.where(
                lane16 < 80,
                pltpu.roll(out[16:32], 32, 1),
                pltpu.roll(out[32:48], 48, 1),
            ),
        )
        gram_scr[16 * s : 16 * s + 16, :] = packed

    gram_scr[256:264, :] = near16[0:8]
    for first, last in ((0, 6), (6, 11), (11, 16)):
        for s in range(first, last):
            make_gram(s)
        rows = pl.ds(16 * first, 16 * (last - first) + 8 * (last == 16))
        send(gram_scr.at[rows, :], gram_pair.at[rows, :], (msg_send, msg_sem), partner)

    def split(source):
        full = jnp.concatenate(
            [source[pl.ds(r, 16, stride=16), :] for r in range(16)], axis=1
        )
        top = full.astype(BF16)
        rest = full - top.astype(F32)
        middle = rest.astype(BF16)
        return [top, middle, (rest - middle.astype(F32)).astype(BF16)]

    right = split(gram_scr)
    wait(gram_pair, msg_sem)
    right = jnp.concatenate(right + split(gram_pair), axis=0)
    wait(w_recv.at[2:], w_sem)
    even_core = lanes((8, 128)) >= 128 * side_v
    by_core = [w_recv[pl.ds(c, 8, stride=2), :] for c in range(2)]
    weights = jnp.where(even_core, by_core[0], by_core[1])
    offset = near16[0:8]
    weighted = [jnp.where(offset == float(o), weights, 0.0) for o in range(REACH)]
    theirs = jnp.where(even_core, by_core[1], by_core[0])
    offset = gram_pair[256:264, :]
    both = [weighted, [jnp.where(offset == float(o), theirs, 0.0) for o in range(REACH)]]
    left = []
    for rows in both:
        half = jnp.concatenate(
            [jnp.where(even_core[:4], x[:4], x[4:]) for x in rows], axis=0
        )
        left += [half[:, :16].astype(BF16)] * 3
    systems = jnp.dot(
        jnp.concatenate(left, axis=1), right, preferred_element_type=F32
    )
    for r in range(16):
        for o in range(REACH):
            near_msg[pl.ds(16 * o + r, 4, stride=64), :] = systems[
                4 * o : 4 * o + 4, 128 * r : 128 * r + 128
            ]

    near = [(o, j) for o in range(REACH) for j in range(4) if (o, j) != (1, 0)]
    near.sort(key=lambda t: -abs(t[0] - 1) - min(t[1], 4 - t[1]))
    for o, j in near:
        there = lax.rem(chip + j, 4)
        send(
            near_msg.at[pl.ds(pl.multiple_of(64 * there + 16 * o, 16), 16), :],
            near_inbox.at[4 * o + j],
            (near_send, near_sem),
            (2 * there + side_v, patch_peer(o - 1)[1]),
        )

    own_copy.wait()
    wait(sci_recv.at[1:], sci_sem)
    for v in range(8):
        for t in range(8):
            sci_scr[128 * t + 16 * v : 128 * t + 16 * v + 16, :] = sci_recv[
                v, :, 128 * t : 128 * t + 128
            ].astype(F32)

    def exposures(s):
        return [sci_scr[pl.ds(128 * t + s, 8, stride=16), :] for t in range(8)]

    sides = [jnp.zeros((8, SIDE), F32) for _ in range(REACH)]
    for s in range(16):
        science = jnp.concatenate(exposures(s), axis=1).astype(BF16)
        out = lax.dot_general(
            science, image_scr[s], second_axes, preferred_element_type=F32
        )
        for o in range(REACH):
            factor = jnp.broadcast_to(weighted[o][:, s : s + 1], (8, SIDE))
            sides[o] = sides[o] + factor * out
    for o in range(REACH):
        side_msg[pl.ds(o, 8, stride=8), :] = jnp.concatenate(
            [sides[o], jnp.zeros((8, 80), F32)], axis=1
        )
        side_msg[pl.ds(4 + o, 8, stride=8), :] = jnp.zeros((8, 128), F32)
    every = [(o, j) for o in range(REACH) for j in range(8) if (o, j) != (1, 0)]
    every.sort(key=lambda t: -abs(t[0] - 1) - (min(t[1], 8 - t[1]) + 1) // 2)
    for o, j in every:
        v = visit_peer(j)[0]
        send(
            side_msg.at[pl.ds(8 * rank(v) + o, 1), :],
            side_near.at[pl.ds(8 * o + j, 1), :],
            (near_side_send, near_side_sem),
            (v, patch_peer(o - 1)[1]),
        )

    total = near_msg[pl.ds(pl.multiple_of(64 * chip + 16, 16), 16), :]
    wait(near_inbox.at[1:], near_sem)
    terms = [total] + [near_inbox[4 * o + j] for o, j in near]
    while len(terms) > 1:
        terms = [a + b for a, b in zip(terms[::2], terms[1::2])]
    total = terms[0]
    inverse = invert(unpack(total[0:8], total[8:16]))
    side_near[8:9, :] = side_msg[pl.ds(8 * rank(me_v) + 1, 1), :]
    wait(near_msg.at[0:31, :], near_side_sem)
    side = jnp.sum(side_near[...], axis=0, keepdims=True)
    side = jnp.where(lanes((1, 128)) < NB, side, 0.0)
    side = jnp.broadcast_to(side, (8, 128))
    across = lanes((8, 128)) - lax.broadcasted_iota(jnp.int32, (8, 128), 0)
    answer = jnp.zeros((8, 128), F32)
    for t in range(6):
        value = jnp.sum(inverse[t] * side, axis=1, keepdims=True)
        answer = answer + jnp.where(across == 8 * t, value, 0.0)
    answer = jnp.sum(answer, axis=0, keepdims=True)
    answer = jnp.where(lanes((1, 128)) < NB, answer, 0.0)
    coef_row[...] = answer
    place = pl.ds(rank(me_v), 1)
    for o, j in every:
        send(
            coef_row,
            coef_box.at[o, place, :],
            (row_send, row_sem),
            (visit_peer(j)[0], patch_peer(1 - o)[1]),
        )
    coef_ref[0] = answer[:, :NB]
    coef_box[1, place, :] = answer
    wait(near_msg.at[0:31, :], row_sem)

    lane8 = lanes((8, 128))

    def fit(s, held):
        choice = jnp.broadcast_to(choice_scr[pl.ds(s, 1), :], (8, 128))
        coefs = coef_box[0]
        for o in range(1, REACH):
            coefs = jnp.where(choice == float(o), coef_box[o], coefs)
        model = jnp.dot(
            coefs[:, :SIDE].astype(BF16), image_scr[s], preferred_element_type=F32
        )
        diff = jnp.concatenate(exposures(s), axis=1) - model
        square = diff * diff
        part = square[:, 0:128]
        for t in range(1, 8):
            part = part + square[:, 128 * t : 128 * t + 128]
        return jnp.where(lane8 == s, jnp.sum(part, axis=1, keepdims=True), held)

    held = lax.fori_loop(0, 16, fit, jnp.zeros((8, 128), F32), unroll=16)
    held = held * weights * (1.0 / 1024.0)
    for v in range(8):
        row = 4 * (v % 2) + v // 2
        residual_ref[v, 0] = held[row : row + 1, :16]

    wait(w_recv.at[2:], w_send)
    wait(sci_recv.at[1:], sci_send)
    wait(gram_pair, msg_send)
    wait(near_inbox.at[1:], near_send)
    wait(near_msg.at[0:31, :], near_side_send)
    wait(near_msg.at[0:31, :], row_send)


def hand_out(coef_ref, residual_ref, coef_out, residual_out, sems):
    copies = [
        pltpu.make_async_copy(coef_ref, coef_out, sems.at[0]),
        pltpu.make_async_copy(residual_ref, residual_out, sems.at[1]),
    ]
    for copy in copies:
        copy.start()
    for copy in copies:
        copy.wait()


def on_device(template, science, weight, stamp_patch, basis_across, basis_down):
    visits = lax.axis_size("visit")
    patches = lax.axis_size("patch")
    vmem = pl.BlockSpec(memory_space=pltpu.VMEM)
    dma = pltpu.SemaphoreType.DMA
    found = pl.pallas_call(
        functools.partial(kernel, visits, patches),
        out_shape=(
            jax.ShapeDtypeStruct((1, 1, NB), F32),
            jax.ShapeDtypeStruct((8, 1, 1, 16), F32),
        ),
        in_specs=[pl.BlockSpec(memory_space=pltpu.HBM)] * 6,
        out_specs=(vmem, vmem),
        scratch_shapes=[
            pltpu.VMEM(template.shape, BF16),
            pltpu.VMEM((TAPS, NB), F32),
            pltpu.VMEM((TAPS, NB), F32),
            pltpu.VMEM(weight.shape, BF16),
            pltpu.VMEM(stamp_patch.shape, jnp.int32),
            pltpu.VMEM((SIDE, 128), F32),
            pltpu.VMEM((SIDE, 128), F32),
            pltpu.VMEM((SIDE * 16, 128), F32),
            pltpu.VMEM((16, 128), F32),
            pltpu.VMEM((8, 128), F32),
            pltpu.VMEM((48, SIDE, 512), BF16),
            pltpu.VMEM((STAMP, SIDE, 512), F32),
            pltpu.VMEM((16, SIDE, 1024), BF16),
            pltpu.VMEM((8, 16, 1024), BF16),
            pltpu.VMEM((1024, 128), F32),
            pltpu.VMEM((16, 128), F32),
            pltpu.VMEM((264, 128), F32),
            pltpu.VMEM((264, 128), F32),
            pltpu.VMEM((64, 128), F32),
            pltpu.VMEM((32, 128), F32),
            pltpu.VMEM((256, 128), F32),
            pltpu.VMEM((16, 16, 128), F32),
            pltpu.VMEM((1, 128), F32),
            pltpu.VMEM((REACH, 8, 128), F32),
        ]
        + [dma, dma((5,))] + [dma] * 12,
        compiler_params=pltpu.CompilerParams(
            collective_id=0, has_side_effects=True, vmem_limit_bytes=32 * 1024 * 1024
        ),
    )(
        *(
            pltpu.with_memory_space_constraint(x, pltpu.HBM)
            for x in (template, basis_across.T, basis_down.T, weight, stamp_patch, science)
        )
    )
    return pl.pallas_call(
        hand_out,
        out_shape=(
            jax.ShapeDtypeStruct((1, 1, NB), F32),
            jax.ShapeDtypeStruct((8, 1, 1, 16), F32),
        ),
        in_specs=[vmem] * 2,
        out_specs=[pl.BlockSpec(memory_space=pl.ANY)] * 2,
        scratch_shapes=[dma((2,))],
    )(*(pltpu.with_memory_space_constraint(x, pltpu.VMEM) for x in found))


def solution(mesh):
    return jax.shard_map(
        on_device,
        mesh=mesh,
        in_specs=(
            P("patch", "visit", None, None),
            P("visit", "patch", None, None, None),
            P("visit", "patch", None, None),
            P("patch", "visit", None),
            P(),
            P(),
        ),
        out_specs=(P("visit", "patch", None), P(None, "patch", "visit", None)),
        check_vma=False,
    )
```

```python
import functools

import jax
import jax.numpy as jnp
from jax import lax
from jax.experimental import pallas as pl
from jax.experimental.pallas import tpu as pltpu
from jax.sharding import PartitionSpec as P

MESH = pl.DeviceIdType.MESH
F32 = jnp.float32
BF16 = jnp.bfloat16

STAMP = 32
TAPS = 17
SIDE = 48
NB = 43
REACH = 4


def lanes(shape):
    return lax.broadcasted_iota(jnp.int32, shape, len(shape) - 1)


def inverse_4x4(m):
    p, q, s = m[0][0], m[0][1], m[1][1]
    i = 1.0 / (p * s - q * q)
    a, b, c = s * i, -q * i, p * i
    e, f, g, h = m[0][2], m[0][3], m[1][2], m[1][3]
    ae, af = a * e + b * g, a * f + b * h
    ce, cf = b * e + c * g, b * f + c * h
    t = m[2][2] - (e * ae + g * ce)
    u = m[2][3] - (e * af + g * cf)
    w = m[3][3] - (f * af + h * cf)
    j = 1.0 / (t * w - u * u)
    x, y, z = w * j, -u * j, t * j
    r00, r01 = -(ae * x + af * y), -(ae * y + af * z)
    r10, r11 = -(ce * x + cf * y), -(ce * y + cf * z)
    n00 = a - (r00 * ae + r01 * af)
    n01 = b - (r00 * ce + r01 * cf)
    n11 = c - (r10 * ce + r11 * cf)
    return (
        (n00, n01, r00, r01),
        (n01, n11, r10, r11),
        (r00, r10, x, y),
        (r01, r11, y, z),
    )


def invert(tiles):
    lane = lanes((8, 128))
    row = lax.broadcasted_iota(jnp.int32, (8, 128), 0)
    tiles = list(tiles)
    for block in range(11):
        first = 4 * block
        home, place = first // 8, first % 8
        rows = [
            jnp.broadcast_to(tiles[home][place + c : place + c + 1, :], (8, 128))
            for c in range(4)
        ]
        pivot = [[None] * 4 for _ in range(4)]
        for r in range(4):
            for c in range(r, 4):
                value = jnp.broadcast_to(rows[r][:, first + c : first + c + 1], (8, 128))
                pivot[r][c] = pivot[c][r] = value
        inverse = inverse_4x4(pivot)
        inside = (lane >= first) & (lane < first + 4)
        rows = [
            jnp.where(inside, jnp.where(lane == first + c, -1.0, 0.0), rows[c])
            for c in range(4)
        ]
        scaled = [
            (inverse[r][0] * rows[0] + inverse[r][1] * rows[1])
            + (inverse[r][2] * rows[2] + inverse[r][3] * rows[3])
            for r in range(4)
        ]
        for t in range(6):
            old = tiles[t]
            cols = [
                jnp.broadcast_to(old[:, first + c : first + c + 1], (8, 128))
                for c in range(4)
            ]
            change = (cols[0] * scaled[0] + cols[1] * scaled[1]) + (
                cols[2] * scaled[2] + cols[3] * scaled[3]
            )
            new = jnp.where(inside, 0.0, old) - change
            if t == home:
                for r in range(4):
                    new = jnp.where(row == place + r, -scaled[r], new)
            tiles[t] = new
    return tiles


def unpack(low, high):
    lane = lanes((8, 128))
    row = lax.broadcasted_iota(jnp.int32, (8, 128), 0)
    tiles = [low, high]
    tiles += [pltpu.roll(x, 96, 1) for x in (low, high)]
    tiles += [pltpu.roll(x, 80, 1) for x in (low, high)]
    full = jnp.concatenate(tiles, axis=0)
    keep = lanes((SIDE, 128)) // 16 >= lax.broadcasted_iota(jnp.int32, (SIDE, 128), 0) // 16
    upper = jnp.where(keep & (lanes((SIDE, 128)) < SIDE), full, 0.0)
    square = jnp.concatenate([upper, jnp.zeros((128 - SIDE, 128), F32)], axis=0)
    flipped = square.T[:SIDE]
    full = jnp.where(keep, upper, flipped)
    tiles = [full[8 * t : 8 * t + 8] for t in range(6)]
    tiles[5] = jnp.where((row == 3) & (lane == NB), 1.0, tiles[5])
    return tiles


def kernel(
    visits,
    patches,
    template_ref,
    across_ref,
    down_ref,
    weight_ref,
    patch_ref,
    science_ref,
    coef_ref,
    residual_ref,
    template_own,
    across_own,
    down_own,
    weight_own,
    patch_own,
    across_scr,
    down_scr,
    turn_scr,
    choice_scr,
    w_own,
    rows_scr,
    wide_scr,
    image_scr,
    sci_recv,
    sci_scr,
    w_recv,
    gram_scr,
    gram_pair,
    side_msg,
    side_near,
    near_msg,
    near_inbox,
    coef_row,
    coef_box,
    own_sem,
    small_sem,
    sci_send,
    sci_sem,
    w_send,
    w_sem,
    msg_send,
    msg_sem,
    near_send,
    near_sem,
    near_side_send,
    near_side_sem,
    row_send,
    row_sem,
):
    me_v = lax.axis_index("visit")
    me_q = lax.axis_index("patch")
    barrier = pltpu.get_barrier_semaphore()

    def visit_peer(step):
        return lax.rem(me_v + step, visits), me_q

    def patch_peer(step):
        return me_v, lax.rem(me_q + step + patches, patches)

    side_v = lax.rem(me_v, 2)
    chip = lax.div(me_v, 2)
    partner = (me_v + 1 - 2 * side_v, me_q)

    def rank(v):
        return 4 * lax.rem(v, 2) + lax.div(v, 2)

    others = range(1, 8)
    around = (-2, -1, 1, 2)

    small = [
        pltpu.make_async_copy(source, target, small_sem.at[n])
        for n, (source, target) in enumerate(
            (
                (template_ref, template_own),
                (across_ref, across_own),
                (down_ref, down_own),
                (weight_ref, weight_own),
                (patch_ref, patch_own),
            )
        )
    ]
    for copy in small:
        copy.start()

    order = (4, 3, 5, 2, 6, 1, 7)
    for peer in [visit_peer(j) for j in order] + [patch_peer(j) for j in around]:
        pl.semaphore_signal(barrier, inc=1, device_id=peer, device_id_type=MESH)

    own_copy = pltpu.make_async_copy(science_ref.at[0, 0, me_v], sci_recv.at[rank(me_v)], own_sem)
    own_copy.start()
    small[0].wait()
    flat = template_own[0, 0].astype(F32)
    for z in range(SIDE):
        turn_scr[16 * z : 16 * z + 16, 0:SIDE] = flat[:, SIDE * z : SIDE * z + SIDE]
    stamps = jnp.concatenate(
        [
            jnp.concatenate(
                [
                    turn_scr[pl.ds(4 * g + s, SIDE, stride=16), :][:, :SIDE]
                    for s in range(4)
                ],
                axis=1,
            )
            for g in range(4)
        ],
        axis=0,
    ).astype(BF16)
    for copy in small[1:]:
        copy.wait()
    w_own[...] = jnp.concatenate(
        [weight_own[0, 0].astype(F32), jnp.zeros((8, 112), F32)], axis=1
    )
    for c in range(2):
        w_recv[pl.ds(2 * rank(me_v) + c, 1), :] = w_own[pl.ds(2 * chip + c, 1), :]
    tap = lax.broadcasted_iota(jnp.int32, (TAPS, 128), 0)
    column = lanes((TAPS, 128)) % STAMP
    backwards = ((column + tap) % STAMP == 0).astype(F32).astype(BF16)
    forwards = (column == tap).astype(F32).astype(BF16)
    nothing5 = jnp.zeros((5, 128), F32)
    across_scr[NB:, :] = nothing5
    first_axes = (((0,), (0,)), ((), ()))
    across_scr[0:NB, :] = lax.dot_general(
        across_own[...].astype(BF16), backwards, first_axes, preferred_element_type=F32
    )
    down_scr[NB:, :] = nothing5
    down_scr[0:NB, :] = lax.dot_general(
        down_own[...].astype(BF16), forwards, first_axes, preferred_element_type=F32
    )
    near = jnp.concatenate([patch_own[0], jnp.zeros((1, 112), jnp.int32)], axis=1)
    near = lax.rem(near - me_q + 1 + patches, patches).astype(F32)
    near16 = jnp.broadcast_to(near, (16, 128))
    diagonal = lanes((16, 128)) == lax.broadcasted_iota(jnp.int32, (16, 128), 0)
    choice_scr[...] = jnp.broadcast_to(
        jnp.sum(jnp.where(diagonal, near16, 0.0), axis=1, keepdims=True), (16, 128)
    )
    def send(source, target, sems, peer):
        pltpu.make_async_remote_copy(
            src_ref=source,
            dst_ref=target,
            send_sem=sems[0],
            recv_sem=sems[1],
            device_id=peer,
            device_id_type=MESH,
        ).start()

    def wait(like, sem):
        pltpu.make_async_copy(like, like, sem).wait()

    shape = (SIDE, 128)
    past = lax.broadcasted_iota(jnp.int32, shape, 0) - lanes(shape) % STAMP
    band = (past >= 0) & (past < TAPS)
    masks = [
        (band & (lanes(shape) // STAMP == s)).astype(F32).astype(BF16) for s in range(4)
    ]
    rows_scr[44:48] = jnp.zeros((4, SIDE, 512), BF16)

    @pl.loop(0, 22, unroll=22)
    def make_rows(pair):
        right = []
        for j in range(2):
            taps = across_scr[pl.ds(2 * pair + j, 1), :]
            table = pltpu.roll(
                jnp.broadcast_to(taps, (STAMP, 128)), 0, 1, stride=1, stride_axis=0
            )
            table = jnp.concatenate([table, table[: SIDE - STAMP]], axis=0).astype(BF16)
            right.append(jnp.concatenate([table * m for m in masks], axis=0))
        right = jnp.concatenate(right, axis=1)
        out = jnp.dot(stamps, right, preferred_element_type=F32).astype(BF16)
        for j in range(2):
            for g in range(4):
                rows_scr[2 * pair + j, :, 128 * g : 128 * g + 128] = out[
                    SIDE * g : SIDE * g + SIDE, 128 * j : 128 * j + 128
                ]

    pl.semaphore_wait(barrier, len(others) + len(around))

    for j in order:
        peer = visit_peer(j)
        send(
            w_own.at[pl.ds(2 * lax.div(peer[0], 2), 2), :],
            w_recv.at[pl.ds(2 * rank(me_v), 2), :],
            (w_send, w_sem),
            peer,
        )
    for j in order:
        peer = visit_peer(j)
        send(
            science_ref.at[0, 0, peer[0]],
            sci_recv.at[rank(me_v)],
            (sci_send, sci_sem),
            peer,
        )

    within = lanes((8, 128)) // STAMP - lax.broadcasted_iota(jnp.int32, (8, 128), 0)
    owner, owner4 = within == 0, within == -4

    @pl.loop(0, 6, unroll=6)
    def make_images(group):
        first = pl.multiple_of(group * 8, 8)
        taps = down_scr[pl.ds(first, 8), :]
        left = jnp.concatenate(
            [jnp.where(owner, taps, 0.0), jnp.where(owner4, taps, 0.0)], axis=1
        )
        left = jnp.concatenate(
            [left]
            + [
                jnp.concatenate(
                    [
                        pltpu.roll(left[:, :128], y, 1),
                        pltpu.roll(left[:, 128:], y, 1),
                    ],
                    axis=1,
                )
                for y in range(1, 16)
            ],
            axis=0,
        ).astype(BF16)
        for half in range(2):
            right = rows_scr[pl.ds(first, 8), 16 * half : 16 * half + 32, :]
            out = jnp.dot(left, right.reshape(256, 512), preferred_element_type=F32)
            wide_scr[16 * half : 16 * half + 16, pl.ds(first, 8), :] = out.reshape(16, 8, 512)

    lane = lanes((SIDE, 128))
    even = lane // STAMP % 2 == 0
    lower = lane < 64

    @pl.loop(0, 8, unroll=8)
    def regroup(quad):
        for g in range(4):
            part = [
                wide_scr[4 * quad + r, :, 128 * g : 128 * g + 128] for r in range(4)
            ]
            for a, b in ((0, 1), (2, 3)):
                x, y = part[a], part[b]
                part[a] = jnp.where(even, x, pltpu.roll(y, 32, 1))
                part[b] = jnp.where(even, pltpu.roll(x, 96, 1), y)
            for a, b in ((0, 2), (1, 3)):
                x, y = part[a], part[b]
                part[a] = jnp.where(lower, x, pltpu.roll(y, 64, 1))
                part[b] = jnp.where(lower, pltpu.roll(x, 64, 1), y)
            for s in range(4):
                image_scr[4 * g + s, :, pl.ds(pl.multiple_of(quad * 128, 128), 128)] = part[
                    s
                ].astype(BF16)

    lane16 = lanes((16, 128))
    second_axes = (((1,), (1,)), ((), ()))

    def make_gram(s):
        image = image_scr[s]
        out = lax.dot_general(image, image, second_axes, preferred_element_type=F32)
        out = jnp.concatenate([out, jnp.zeros((SIDE, 80), F32)], axis=1)
        packed = jnp.where(
            lane16 < 48,
            out[0:16],
            jnp.where(
                lane16 < 80,
                pltpu.roll(out[16:32], 32, 1),
                pltpu.roll(out[32:48], 48, 1),
            ),
        )
        gram_scr[16 * s : 16 * s + 16, :] = packed

    gram_scr[256:264, :] = near16[0:8]
    for first, last in ((0, 8), (8, 14), (14, 16)):
        for s in range(first, last):
            make_gram(s)
        rows = pl.ds(16 * first, 16 * (last - first) + 8 * (last == 16))
        send(gram_scr.at[rows, :], gram_pair.at[rows, :], (msg_send, msg_sem), partner)

    def split(source):
        full = jnp.concatenate(
            [source[pl.ds(r, 16, stride=16), :] for r in range(16)], axis=1
        )
        top = full.astype(BF16)
        rest = full - top.astype(F32)
        middle = rest.astype(BF16)
        return [top, middle, (rest - middle.astype(F32)).astype(BF16)]

    right = split(gram_scr)
    wait(gram_pair, msg_sem)
    right = jnp.concatenate(right + split(gram_pair), axis=0)
    wait(w_recv.at[2:], w_sem)
    even_core = lanes((8, 128)) >= 128 * side_v
    by_core = [w_recv[pl.ds(c, 8, stride=2), :] for c in range(2)]
    weights = jnp.where(even_core, by_core[0], by_core[1])
    offset = near16[0:8]
    weighted = [jnp.where(offset == float(o), weights, 0.0) for o in range(REACH)]
    theirs = jnp.where(even_core, by_core[1], by_core[0])
    offset = gram_pair[256:264, :]
    both = [weighted, [jnp.where(offset == float(o), theirs, 0.0) for o in range(REACH)]]
    left = []
    for rows in both:
        half = jnp.concatenate(
            [jnp.where(even_core[:4], x[:4], x[4:]) for x in rows], axis=0
        )
        left += [half[:, :16].astype(BF16)] * 3
    systems = jnp.dot(
        jnp.concatenate(left, axis=1), right, preferred_element_type=F32
    )
    for r in range(16):
        for o in range(REACH):
            near_msg[pl.ds(16 * o + r, 4, stride=64), :] = systems[
                4 * o : 4 * o + 4, 128 * r : 128 * r + 128
            ]

    near = [(o, j) for o in range(REACH) for j in range(4) if (o, j) != (1, 0)]
    near.sort(key=lambda t: -abs(t[0] - 1) - min(t[1], 4 - t[1]))
    for o, j in near:
        there = lax.rem(chip + j, 4)
        send(
            near_msg.at[pl.ds(pl.multiple_of(64 * there + 16 * o, 16), 16), :],
            near_inbox.at[4 * o + j],
            (near_send, near_sem),
            (2 * there + side_v, patch_peer(o - 1)[1]),
        )

    own_copy.wait()
    wait(sci_recv.at[1:], sci_sem)
    for v in range(8):
        for t in range(8):
            sci_scr[128 * t + 16 * v : 128 * t + 16 * v + 16, :] = sci_recv[
                v, :, 128 * t : 128 * t + 128
            ].astype(F32)

    def exposures(s):
        return [sci_scr[pl.ds(128 * t + s, 8, stride=16), :] for t in range(8)]

    sides = [jnp.zeros((8, SIDE), F32) for _ in range(REACH)]
    for s in range(16):
        science = jnp.concatenate(exposures(s), axis=1).astype(BF16)
        out = lax.dot_general(
            science, image_scr[s], second_axes, preferred_element_type=F32
        )
        for o in range(REACH):
            factor = jnp.broadcast_to(weighted[o][:, s : s + 1], (8, SIDE))
            sides[o] = sides[o] + factor * out
    for o in range(REACH):
        side_msg[pl.ds(o, 8, stride=8), :] = jnp.concatenate(
            [sides[o], jnp.zeros((8, 80), F32)], axis=1
        )
        side_msg[pl.ds(4 + o, 8, stride=8), :] = jnp.zeros((8, 128), F32)
    every = [(o, j) for o in range(REACH) for j in range(8) if (o, j) != (1, 0)]
    every.sort(key=lambda t: -abs(t[0] - 1) - (min(t[1], 8 - t[1]) + 1) // 2)
    for o, j in every:
        v = visit_peer(j)[0]
        send(
            side_msg.at[pl.ds(8 * rank(v) + o, 1), :],
            side_near.at[pl.ds(8 * o + j, 1), :],
            (near_side_send, near_side_sem),
            (v, patch_peer(o - 1)[1]),
        )

    total = near_msg[pl.ds(pl.multiple_of(64 * chip + 16, 16), 16), :]
    wait(near_inbox.at[1:], near_sem)
    terms = [total] + [near_inbox[4 * o + j] for o, j in near]
    while len(terms) > 1:
        terms = [a + b for a, b in zip(terms[::2], terms[1::2])]
    total = terms[0]
    inverse = invert(unpack(total[0:8], total[8:16]))
    side_near[8:9, :] = side_msg[pl.ds(8 * rank(me_v) + 1, 1), :]
    wait(near_msg.at[0:31, :], near_side_sem)
    side = jnp.sum(side_near[...], axis=0, keepdims=True)
    side = jnp.where(lanes((1, 128)) < NB, side, 0.0)
    side = jnp.broadcast_to(side, (8, 128))
    across = lanes((8, 128)) - lax.broadcasted_iota(jnp.int32, (8, 128), 0)
    answer = jnp.zeros((8, 128), F32)
    for t in range(6):
        value = jnp.sum(inverse[t] * side, axis=1, keepdims=True)
        answer = answer + jnp.where(across == 8 * t, value, 0.0)
    answer = jnp.sum(answer, axis=0, keepdims=True)
    answer = jnp.where(lanes((1, 128)) < NB, answer, 0.0)
    coef_row[...] = answer
    place = pl.ds(rank(me_v), 1)
    for o, j in every:
        send(
            coef_row,
            coef_box.at[o, place, :],
            (row_send, row_sem),
            (visit_peer(j)[0], patch_peer(1 - o)[1]),
        )
    coef_ref[0] = answer[:, :NB]
    coef_box[1, place, :] = answer
    wait(near_msg.at[0:31, :], row_sem)

    lane8 = lanes((8, 128))

    def fit(s, held):
        choice = jnp.broadcast_to(choice_scr[pl.ds(s, 1), :], (8, 128))
        coefs = coef_box[0]
        for o in range(1, REACH):
            coefs = jnp.where(choice == float(o), coef_box[o], coefs)
        model = jnp.dot(
            coefs[:, :SIDE].astype(BF16), image_scr[s], preferred_element_type=F32
        )
        diff = jnp.concatenate(exposures(s), axis=1) - model
        square = diff * diff
        part = square[:, 0:128]
        for t in range(1, 8):
            part = part + square[:, 128 * t : 128 * t + 128]
        return jnp.where(lane8 == s, jnp.sum(part, axis=1, keepdims=True), held)

    held = lax.fori_loop(0, 16, fit, jnp.zeros((8, 128), F32), unroll=16)
    held = held * weights * (1.0 / 1024.0)
    for v in range(8):
        row = 4 * (v % 2) + v // 2
        residual_ref[v, 0] = held[row : row + 1, :16]

    wait(w_recv.at[2:], w_send)
    wait(sci_recv.at[1:], sci_send)
    wait(gram_pair, msg_send)
    wait(near_inbox.at[1:], near_send)
    wait(near_msg.at[0:31, :], near_side_send)
    wait(near_msg.at[0:31, :], row_send)


def hand_out(coef_ref, residual_ref, coef_out, residual_out, sems):
    copies = [
        pltpu.make_async_copy(coef_ref, coef_out, sems.at[0]),
        pltpu.make_async_copy(residual_ref, residual_out, sems.at[1]),
    ]
    for copy in copies:
        copy.start()
    for copy in copies:
        copy.wait()


def on_device(template, science, weight, stamp_patch, basis_across, basis_down):
    visits = lax.axis_size("visit")
    patches = lax.axis_size("patch")
    vmem = pl.BlockSpec(memory_space=pltpu.VMEM)
    dma = pltpu.SemaphoreType.DMA
    found = pl.pallas_call(
        functools.partial(kernel, visits, patches),
        out_shape=(
            jax.ShapeDtypeStruct((1, 1, NB), F32),
            jax.ShapeDtypeStruct((8, 1, 1, 16), F32),
        ),
        in_specs=[pl.BlockSpec(memory_space=pltpu.HBM)] * 6,
        out_specs=(vmem, vmem),
        scratch_shapes=[
            pltpu.VMEM(template.shape, BF16),
            pltpu.VMEM((TAPS, NB), F32),
            pltpu.VMEM((TAPS, NB), F32),
            pltpu.VMEM(weight.shape, BF16),
            pltpu.VMEM(stamp_patch.shape, jnp.int32),
            pltpu.VMEM((SIDE, 128), F32),
            pltpu.VMEM((SIDE, 128), F32),
            pltpu.VMEM((SIDE * 16, 128), F32),
            pltpu.VMEM((16, 128), F32),
            pltpu.VMEM((8, 128), F32),
            pltpu.VMEM((48, SIDE, 512), BF16),
            pltpu.VMEM((STAMP, SIDE, 512), F32),
            pltpu.VMEM((16, SIDE, 1024), BF16),
            pltpu.VMEM((8, 16, 1024), BF16),
            pltpu.VMEM((1024, 128), F32),
            pltpu.VMEM((16, 128), F32),
            pltpu.VMEM((264, 128), F32),
            pltpu.VMEM((264, 128), F32),
            pltpu.VMEM((64, 128), F32),
            pltpu.VMEM((32, 128), F32),
            pltpu.VMEM((256, 128), F32),
            pltpu.VMEM((16, 16, 128), F32),
            pltpu.VMEM((1, 128), F32),
            pltpu.VMEM((REACH, 8, 128), F32),
        ]
        + [dma, dma((5,))] + [dma] * 12,
        compiler_params=pltpu.CompilerParams(
            collective_id=0, has_side_effects=True, vmem_limit_bytes=32 * 1024 * 1024
        ),
    )(
        *(
            pltpu.with_memory_space_constraint(x, pltpu.HBM)
            for x in (template, basis_across.T, basis_down.T, weight, stamp_patch, science)
        )
    )
    return pl.pallas_call(
        hand_out,
        out_shape=(
            jax.ShapeDtypeStruct((1, 1, NB), F32),
            jax.ShapeDtypeStruct((8, 1, 1, 16), F32),
        ),
        in_specs=[vmem] * 2,
        out_specs=[pl.BlockSpec(memory_space=pl.ANY)] * 2,
        scratch_shapes=[dma((2,))],
    )(*(pltpu.with_memory_space_constraint(x, pltpu.VMEM) for x in found))


def solution(mesh):
    return jax.shard_map(
        on_device,
        mesh=mesh,
        in_specs=(
            P("patch", "visit", None, None),
            P("visit", "patch", None, None, None),
            P("visit", "patch", None, None),
            P("patch", "visit", None),
            P(),
            P(),
        ),
        out_specs=(P("visit", "patch", None), P(None, "patch", "visit", None)),
        check_vma=False,
    )
```
